32 devices in a mesh: vel: 8 (over y, x, core), gx: 4 (over z).
Axes of the slice: x: 2, y: 2, z: 4, core: 2. Of those that a mesh axis runs over, the one named last changes fastest.
Arguments:
- distribution: float32 [4096, 8192], P('vel', 'gx'), as said below
- wall_mask: int32 [16, 512], replicated, may hold values 0 or 1
- boundary_kind: int32 [2, 512], replicated, may hold values from 0 to 1
- inflow: float32 [4096], P('vel'), may hold values from 0.5 to 3
Outputs:
- evolved: float32 [4096, 8192], P('vel', 'gx')
The draws below stay inside these ranges and needn't reach their ends.
Inputs may be any that keep to these rules, and one draw needn't show every extreme that they name: `distribution`: every entry is positive. `wall_mask`: 1 marks a solid cell. `boundary_kind`: 0 is an outflow face, 1 an inflow face.
All inputs are finite; a program needn't handle non-finite values.
Results may differ from the reference program's by a relative error of at most 0.0003.
Values sent between devices are 32-bit elements; how exact they have to be, the bound alone decides.
A program may use at most 128 MiB of HBM per device.

```python
import math
import jax
import jax.numpy as jnp
from jax import lax

VS = 16
NY = 16
NZ = 32
STEPS = 3
NV = 4096
NX = 16
NYZ = 512
CELLS = 8192


def draw_distribution(key, part):
    first, second = jax.random.split(jax.random.fold_in(key, 7), 2)
    ramp = (jnp.arange(NV) // (VS * VS)).astype(jnp.float32) / (VS - 1)
    base = jnp.exp(jax.random.uniform(first, (NV, CELLS), jnp.float32, -0.7, 0.7))
    row_scale = 1.0 + 2.0 * ramp
    cell_scale = jnp.exp(jax.random.uniform(second, (CELLS,), jnp.float32, math.log(0.3), math.log(3.0)))
    return base * row_scale[:, None] * cell_scale[None, :]


def plant(values, key, least, high):
    dims = values.shape
    index_at = [jax.random.randint(jax.random.fold_in(key, axis), (), 0, dims[axis]) for axis in range(len(dims))]
    values = values.at[tuple(index_at)].set(least)
    longest = dims.index(max(dims))
    index_at[longest] = (index_at[longest] + 1) % dims[longest]
    return values.at[tuple(index_at)].set(high)


def shard_levels(rng, dims, cuts, least, high):
    def one(axis_at, parts):
        steps = jax.random.uniform(jax.random.fold_in(jax.random.fold_in(rng, 6), axis_at), (parts,), jnp.float32, least / len(cuts), high / len(cuts))
        return jnp.repeat(jnp.exp(steps), dims[axis_at] // parts).reshape((-1,) + (1,) * (len(dims) - axis_at - 1))

    gain = one(*cuts[0])
    for cut in cuts[1:]:
        gain = gain * one(*cut)
    return gain


def setup_inputs(seed: int = 0) -> dict:
    arg_keys = jax.random.split(jax.random.key(seed), 5)
    return {
        "distribution": draw_distribution(jax.random.fold_in(arg_keys[4], 71), 0),
        "wall_mask": plant((jax.random.randint(arg_keys[1], (NX, NYZ), 0, 8) < 1).astype(jnp.int32), jax.random.fold_in(arg_keys[1], 1), 0, 1),
        "boundary_kind": plant(jax.random.randint(arg_keys[2], (2, NYZ), 0, 2), jax.random.fold_in(arg_keys[2], 1), 0, 1).astype(jnp.int32),
        "inflow": jnp.clip(jnp.exp(math.log(3.0) - 1.7917595 * jax.random.uniform(arg_keys[3], (NV,), jnp.float32) ** shard_levels(arg_keys[3], (NV,), ((0, 8),), -0.2, 0.2)), 0.5, 3.0),
    }


vel_limit = 4.5
time_step = 0.075
relax_rate = 0.6
viscous_thermal_ratio = 0.6666667


def velocity_rows(lattice_lines):
    square = VS * VS
    half = square // 2
    across = lattice_lines // square
    rest = lattice_lines % square
    upper = rest // half
    inner = rest % half
    along = jnp.where(upper == 1, VS // 2 + inner // VS, VS // 2 - 1 - inner // VS)
    depth = inner % VS
    spacing = 2.0 * vel_limit / VS

    def coord(index):
        return -vel_limit + (index.astype(jnp.float32) + 0.5) * spacing

    return coord(along), coord(across), coord(depth)


def poly_basis(speed_x, speed_y, speed_z):
    energy = speed_x * speed_x + speed_y * speed_y + speed_z * speed_z
    return jnp.stack([jnp.ones_like(speed_x), speed_x, speed_y, speed_z,
                      speed_x * speed_x, speed_y * speed_y, speed_z * speed_z,
                      speed_x * speed_y, speed_x * speed_z, speed_y * speed_z,
                      energy * speed_x, energy * speed_y, energy * speed_z], axis=1)


def exp_basis(speed_x, speed_y, speed_z):
    energy = speed_x * speed_x + speed_y * speed_y + speed_z * speed_z
    return jnp.stack([jnp.ones_like(speed_x), speed_x, speed_y, speed_z, energy], axis=1)


def shakhov_coefficients(moments):
    particle_concentration = moments[0]
    mean_drift_first = moments[1] / particle_concentration
    mean_drift_second = moments[2] / particle_concentration
    mean_drift_third_dir = moments[3] / particle_concentration
    second = moments[4:10]
    motion_work_content = mean_drift_first * mean_drift_first + mean_drift_second * mean_drift_second + mean_drift_third_dir * mean_drift_third_dir
    pressure_diagonal_sum = second[0] + second[1] + second[2]
    thermal_level = (pressure_diagonal_sum / particle_concentration - motion_work_content) / 3.0
    press_x = second[0] * mean_drift_first + second[3] * mean_drift_second + second[4] * mean_drift_third_dir
    press_y = second[3] * mean_drift_first + second[1] * mean_drift_second + second[5] * mean_drift_third_dir
    press_z = second[4] * mean_drift_first + second[5] * mean_drift_second + second[2] * mean_drift_third_dir
    heat_x = 0.5 * (moments[10] - 2.0 * press_x - mean_drift_first * pressure_diagonal_sum + 2.0 * particle_concentration * motion_work_content * mean_drift_first)
    heat_y = 0.5 * (moments[11] - 2.0 * press_y - mean_drift_second * pressure_diagonal_sum + 2.0 * particle_concentration * motion_work_content * mean_drift_second)
    heat_z = 0.5 * (moments[12] - 2.0 * press_z - mean_drift_third_dir * pressure_diagonal_sum + 2.0 * particle_concentration * motion_work_content * mean_drift_third_dir)
    heat_diffusivity_coef = (1.0 - viscous_thermal_ratio) / (5.0 * particle_concentration * thermal_level * thermal_level)
    quadrature_scale = heat_diffusivity_coef / thermal_level
    mixed = mean_drift_first * heat_x + mean_drift_second * heat_y + mean_drift_third_dir * heat_z
    foremost_dimension = jnp.log(particle_concentration) - 1.5 * jnp.log(2.0 * jnp.pi * thermal_level) - motion_work_content / (2.0 * thermal_level)
    lattice_lines = [foremost_dimension, mean_drift_first / thermal_level, mean_drift_second / thermal_level, mean_drift_third_dir / thermal_level, -0.5 / thermal_level,
            1.0 - quadrature_scale * mixed * motion_work_content + 5.0 * heat_diffusivity_coef * mixed,
            quadrature_scale * (heat_x * motion_work_content + 2.0 * mixed * mean_drift_first) - 5.0 * heat_diffusivity_coef * heat_x,
            quadrature_scale * (heat_y * motion_work_content + 2.0 * mixed * mean_drift_second) - 5.0 * heat_diffusivity_coef * heat_y,
            quadrature_scale * (heat_z * motion_work_content + 2.0 * mixed * mean_drift_third_dir) - 5.0 * heat_diffusivity_coef * heat_z,
            -2.0 * quadrature_scale * heat_x * mean_drift_first - quadrature_scale * mixed,
            -2.0 * quadrature_scale * heat_y * mean_drift_second - quadrature_scale * mixed,
            -2.0 * quadrature_scale * heat_z * mean_drift_third_dir - quadrature_scale * mixed,
            -2.0 * quadrature_scale * (heat_x * mean_drift_second + heat_y * mean_drift_first),
            -2.0 * quadrature_scale * (heat_x * mean_drift_third_dir + heat_z * mean_drift_first),
            -2.0 * quadrature_scale * (heat_y * mean_drift_third_dir + heat_z * mean_drift_second),
            quadrature_scale * heat_x, quadrature_scale * heat_y, quadrature_scale * heat_z]
    return jnp.stack(lattice_lines, axis=0)


def relax(moved, coefficients, expo_rows, poly_rows):
    power = jnp.dot(expo_rows, coefficients[0:5], precision=lax.Precision.HIGHEST)
    shape = jnp.dot(poly_rows, coefficients[5:18], precision=lax.Precision.HIGHEST)
    return moved + relax_rate * (jnp.exp(power) * shape - moved)


def reference(distribution, wall_mask, boundary_kind, inflow):
    rows_all = jnp.arange(NV, dtype=jnp.int32)
    speed_x, speed_y, speed_z = velocity_rows(rows_all)
    poly = poly_basis(speed_x, speed_y, speed_z)
    expo = exp_basis(speed_x, speed_y, speed_z)
    weight = (2.0 * vel_limit / VS) ** 3
    openness = (1 - wall_mask).astype(jnp.float32).reshape(NX, NY, NZ)
    open_pad = jnp.pad(openness, ((1, 1), (0, 0), (0, 0)), constant_values=1.0)
    low_in = (boundary_kind[0] == 1).reshape(NY, NZ)
    high_in = (boundary_kind[1] == 1).reshape(NY, NZ)
    block = VS * VS
    count = NV // block

    def split(array):
        return array.reshape((count, block) + array.shape[1:])

    def transport(pieces):
        values, along_x, along_y, along_z, entering = pieces
        cube = values.reshape(block, NX, NY, NZ)
        low_ghost = jnp.where(low_in[None], entering[:, None, None], cube[:, 0])
        high_ghost = jnp.where(high_in[None], entering[:, None, None], cube[:, NX - 1])
        extended = jnp.concatenate([low_ghost[:, None], cube, high_ghost[:, None]], axis=1)
        speed = along_x[:, None, None, None]
        upwind = jnp.where(speed > 0, extended[:, :-1], extended[:, 1:])
        flux = speed * upwind * (open_pad[:-1] * open_pad[1:])
        change = flux[:, 1:] - flux[:, :-1]
        speed = along_y[:, None, None, None]
        upwind = jnp.where(speed > 0, cube[:, :, :-1], cube[:, :, 1:])
        flux = speed * upwind * (openness[:, :-1] * openness[:, 1:])
        flux = jnp.pad(flux, ((0, 0), (0, 0), (1, 1), (0, 0)))
        change = change + (flux[:, :, 1:] - flux[:, :, :-1])
        speed = along_z[:, None, None, None]
        upwind = jnp.where(speed > 0, cube[:, :, :, :-1], cube[:, :, :, 1:])
        flux = speed * upwind * (openness[:, :, :-1] * openness[:, :, 1:])
        flux = jnp.pad(flux, ((0, 0), (0, 0), (0, 0), (1, 1)))
        change = change + (flux[:, :, :, 1:] - flux[:, :, :, :-1])
        return (cube - time_step * change).reshape(block, CELLS)

    def accumulate(total, pieces):
        values, poly_block = pieces
        return total + jnp.dot(poly_block.T, values, precision=lax.Precision.HIGHEST), None

    state = split(distribution)
    for step in range(STEPS):
        moved = lax.map(transport, (state, split(speed_x), split(speed_y), split(speed_z), split(inflow)))
        total, unused = lax.scan(accumulate, jnp.zeros((13, CELLS), jnp.float32), (moved, split(poly)))
        coefficients = shakhov_coefficients(weight * total)

        def relax_block(pieces):
            values, expo_block, poly_block = pieces
            return relax(values, coefficients, expo_block, poly_block)

        state = lax.map(relax_block, (moved, split(expo), split(poly)))
    return state.reshape(NV, CELLS)
```

```python
import math

import jax
import jax.numpy as jnp
from jax import lax
from jax.experimental import pallas as pl
from jax.experimental.pallas import tpu as pltpu
from jax.sharding import PartitionSpec as P

VS = 16
NY = 16
NZ = 32
STEPS = 3
LANES = 128
FEATURES = 16
TERMS = 3
COEFS = 24

vel_limit = 4.5
time_step = 0.075
relax_rate = 0.6
viscous_thermal_ratio = 0.6666667
spacing = 2.0 * vel_limit / VS
unit = spacing / 2.0
MESH = pl.DeviceIdType.MESH
F32 = jnp.float32
BF16 = jnp.bfloat16


def features(index, cx, cy, cz):
    energy = cx * cx + cy * cy + cz * cz

    def high(value):
        return jnp.floor(value * (1.0 / 64.0)) * 64.0

    cubes = [energy * cx, energy * cy, energy * cz]
    rows = [jnp.ones_like(cx), cx, cy, cz, cx * cx, cy * cy, cz * cz, cx * cy, cx * cz, cy * cz]
    rows += [high(c) for c in cubes]
    rows += [c - high(c) for c in cubes]
    out = rows[0]
    for k in range(1, FEATURES):
        out = jnp.where(index == k, rows[k], out)
    return out


def shakhov_rows(moments):
    weight = spacing**3
    degree = [0, 1, 1, 1, 2, 2, 2, 2, 2, 2, 3, 3, 3]
    m = [moments[k : k + 1] for k in range(FEATURES)]
    m = m[:10] + [m[10 + a] + m[13 + a] for a in range(3)]
    m = [row * (weight * unit**d) for row, d in zip(m, degree)]
    n = m[0]
    inv_n = 1.0 / n
    u = [m[1] * inv_n, m[2] * inv_n, m[3] * inv_n]
    xx, yy, zz, xy, xz, yz = m[4:10]
    uu = u[0] * u[0] + u[1] * u[1] + u[2] * u[2]
    tr = xx + yy + zz
    temp = (tr * inv_n - uu) / 3.0
    press = [
        xx * u[0] + xy * u[1] + xz * u[2],
        xy * u[0] + yy * u[1] + yz * u[2],
        xz * u[0] + yz * u[1] + zz * u[2],
    ]
    q = [0.5 * (m[10 + a] - 2.0 * press[a] - u[a] * tr + 2.0 * n * uu * u[a]) for a in range(3)]
    inv_t = 1.0 / temp
    kappa = (1.0 - viscous_thermal_ratio) / (5.0 * n * temp * temp)
    s = kappa * inv_t
    uq = u[0] * q[0] + u[1] * q[1] + u[2] * q[2]
    first = jnp.log(n) - 1.5 * jnp.log(2.0 * math.pi * temp) - uu * (0.5 * inv_t)
    quad = -0.5 * inv_t
    expo = [first, u[0] * inv_t, u[1] * inv_t, u[2] * inv_t, quad, quad, quad]
    expo = [row * (math.log2(math.e) * unit**d) for row, d in zip(expo, [0, 1, 1, 1, 2, 2, 2])]
    poly = [1.0 - s * uq * uu + 5.0 * kappa * uq]
    poly += [s * (q[a] * uu + 2.0 * uq * u[a]) - 5.0 * kappa * q[a] for a in range(3)]
    poly += [-2.0 * s * q[a] * u[a] - s * uq for a in range(3)]
    poly += [-2.0 * s * (q[a] * u[b] + q[b] * u[a]) for a, b in ((0, 1), (0, 2), (1, 2))]
    poly += [s * q[a] for a in range(3)]
    poly = [row * (relax_rate * unit**d) for row, d in zip(poly, degree)]
    poly += poly[10:13]
    return jnp.concatenate(expo + [jnp.zeros_like(n)] + poly, axis=0)


def make_kernel(n_vel, n_gx, blocks, half, depth, section):
    G = STEPS
    Q = depth + G
    cells = depth * section
    piece = cells // n_vel
    tiles = section // LANES
    wide = 2 * LANES
    zh_rows = VS // 2

    def plane_of(h, q):
        return q - G if h == 1 else depth - 1 + G - q

    def kernel(
        dist, wall, kind, inflow, out,
        S, M, H, PART, GOT, CO, CG, PHI, L, RP, RS, INF,
        in_sem, out_sem, hs_sem, hr_sem, ps_sem, pr_sem, cs_sem, cr_sem, gs_sem, gr_sem,
    ):
        me = lax.axis_index("vel")
        pos = lax.axis_index("gx")
        has_left = pos > 0
        has_right = pos < n_gx - 1
        has_up = [has_right, has_left]
        has_down = [has_left, has_right]
        up = [pos + 1, pos - 1]
        down = [pos - 1, pos + 1]

        def columns(x):
            return pl.ds(x * section, section)

        loads = {}
        for q in range(Q - 1, G - 1, -1):
            for h in range(2):
                copy = pltpu.make_async_copy(
                    dist.at[:, h, :, columns(plane_of(h, q))], S.at[h, q], in_sem.at[h, q - G]
                )
                copy.start()
                loads[h, q] = copy

        barrier = pltpu.get_barrier_semaphore()
        for d in range(1, n_vel):
            pl.semaphore_signal(
                barrier, inc=1, device_id={"vel": lax.rem(me + d, n_vel)}, device_id_type=MESH
            )
        for h in range(2):
            @pl.when(has_down[h])
            def _(h=h):
                pl.semaphore_signal(barrier, inc=1, device_id={"gx": down[h]}, device_id_type=MESH)
        met = n_vel - 1 + has_left.astype(jnp.int32) + has_right.astype(jnp.int32)
        pl.semaphore_wait(barrier, met)

        def halo(h, k):
            x = depth - 1 - k if h == 1 else k
            return pltpu.make_async_remote_copy(
                src_ref=dist.at[:, h, :, columns(x)],
                dst_ref=S.at[h, G - 1 - k],
                send_sem=hs_sem.at[h, k],
                recv_sem=hr_sem.at[h, k],
                device_id={"gx": down[h]},
                device_id_type=MESH,
            )

        def start_halo(k):
            for h in range(2):
                @pl.when(has_down[h])
                def _(h=h):
                    halo(h, k).start()

        def finish_halo_send(k):
            for h in range(2):
                @pl.when(has_down[h])
                def _(h=h):
                    halo(h, k).wait_send()

        start_halo(0)

        first_iy = me * blocks
        lane = lax.broadcasted_iota(jnp.int32, (1, section), 1)
        y_at = lane // NZ
        z_at = lane % NZ
        vy_up = first_iy >= VS // 2
        n_planes = wall.shape[0]

        def openness(x):
            at = pos * depth + x
            row = wall[pl.ds(jnp.clip(at, 0, n_planes - 1), 1), :]
            inside = jnp.logical_and(at >= 0, at < n_planes)
            return jnp.where(inside, (1 - row).astype(F32), 1.0)

        for h in range(2):
            way = 1 if h == 1 else -1
            for q in range(1, Q):
                x = plane_of(h, q)
                o = openness(x)
                x_in = o * openness(x - way)
                x_out = o * openness(x + way)
                y_hi = jnp.where(y_at < NY - 1, o * pltpu.roll(o, section - NZ, 1), 0.0)
                y_lo = jnp.where(y_at > 0, o * pltpu.roll(o, NZ, 1), 0.0)
                z_hi = jnp.where(z_at < NZ - 1, o * pltpu.roll(o, section - 1, 1), 0.0)
                z_lo = jnp.where(z_at > 0, o * pltpu.roll(o, 1, 1), 0.0)
                y_in = jnp.where(vy_up, y_lo, y_hi)
                y_out = jnp.where(vy_up, y_hi, y_lo)
                rows = [x_in, x_out, y_in, y_out, z_hi, z_lo, z_lo, z_hi]
                H[h, q] = jnp.concatenate([r * time_step for r in rows], axis=0)

        for h in range(2):
            sign = 1.0 if h == 1 else -1.0
            shape = (FEATURES, blocks * half)
            r = lax.broadcasted_iota(jnp.int32, shape, 1)
            index = lax.broadcasted_iota(jnp.int32, shape, 0)
            cx = sign * (2 * ((r % half) // VS) + 1).astype(F32)
            cz = (2 * (r % VS) - (VS - 1)).astype(F32)
            cy = (2 * (first_iy + r // half) - (VS - 1)).astype(F32)
            PHI[h] = features(index, cx, cy, cz).astype(BF16)
            shape = (half, FEATURES * TERMS)
            r = lax.broadcasted_iota(jnp.int32, shape, 0)
            index = lax.broadcasted_iota(jnp.int32, shape, 1) % FEATURES
            cx = sign * (2 * (r // VS) + 1).astype(F32)
            cz = (2 * (r % VS) - (VS - 1)).astype(F32)
            for b in range(blocks):
                cy = jnp.full(shape, 2 * (first_iy + b) - (VS - 1), jnp.int32).astype(F32)
                L[h, b] = features(index, cx, cy, cz).astype(BF16)
                row = inflow[2 * b + h : 2 * b + h + 1, :]
                INF[h, b] = jnp.broadcast_to(row, (half, half)).T

        lane_t = lax.broadcasted_iota(jnp.int32, (zh_rows, LANES), 1)
        sub = lax.broadcasted_iota(jnp.int32, (zh_rows, LANES), 0).astype(F32)
        y_take = jnp.where(vy_up, LANES - NZ, 0)
        from_next = jnp.logical_and(lane_t >= y_take, lane_t < y_take + NZ)
        y_shift = jnp.where(vy_up, NZ, LANES - NZ)
        t_step = jnp.where(vy_up, tiles - 1, 1)

        def transport(h_list, q0, nq):
            per_h = nq * blocks * tiles

            def body(j, carry):
                if len(h_list) == 2:
                    h = j // per_h
                else:
                    h = h_list[0]
                rest = j % per_h
                q = q0 + rest // (blocks * tiles)
                b = (rest // tiles) % blocks
                t = rest % tiles
                at = pl.ds(pl.multiple_of(t * LANES, LANES), LANES)
                t_next = (t + t_step) % tiles
                at_next = pl.ds(pl.multiple_of(t_next * LANES, LANES), LANES)
                speed_y = jnp.abs(-vel_limit + ((first_iy + b).astype(F32) + 0.5) * spacing)

                def face(k):
                    return jnp.broadcast_to(H[h, q, k : k + 1, at], (zh_rows, LANES))

                x_in, x_out = face(0), face(1)
                y_in = face(2) * speed_y
                y_keep = 1.0 - face(3) * speed_y
                for zh in range(2):
                    if zh == 0:
                        speed_z = vel_limit - (sub + 0.5) * spacing
                    else:
                        speed_z = (sub + 0.5) * spacing
                    z_in = face(4 + 2 * zh) * speed_z
                    keep = y_keep - face(5 + 2 * zh) * speed_z
                    for i in range(half // VS):
                        rows = pl.ds(i * VS + zh * zh_rows, zh_rows)
                        speed_x = (i + 0.5) * spacing
                        f = S[h, q, b, rows, at]
                        before = S[h, q - 1, b, rows, at]
                        beside = S[h, q, b, rows, at_next]
                        f_y = pltpu.roll(jnp.where(from_next, beside, f), y_shift, 1)
                        f_z = pltpu.roll(f, 1 if zh == 1 else LANES - 1, 1)
                        moved = f * (keep - x_out * speed_x) + before * (x_in * speed_x)
                        moved = moved + (f_y * y_in + f_z * z_in)
                        M[h, q, b, rows, at] = moved
                return carry

            lax.fori_loop(0, len(h_list) * per_h, body, 0)

        def moments(h, q):
            halves = []
            for c in range(section // wide):
                value = M[h, q, :, :, c * wide : (c + 1) * wide].reshape(blocks * half, wide)
                hi = value.astype(BF16)
                lo = (value - hi.astype(F32)).astype(BF16)
                phi = PHI[h]
                halves.append(
                    jnp.dot(phi, hi, preferred_element_type=F32)
                    + jnp.dot(phi, lo, preferred_element_type=F32)
                )
            return halves

        def load_coefficients(rows):
            terms = []
            rest = rows
            for j in range(TERMS):
                term = rest.astype(BF16)
                terms.append(term)
                rest = rest - term.astype(F32)
            for j in range(TERMS):
                at = slice(j * FEATURES, (j + 1) * FEATURES)
                RP[at, :] = jnp.concatenate(
                    [terms[j][0:8], jnp.zeros((8, section), BF16)], axis=0
                )
                RS[at, :] = terms[j][8:COEFS]

        def relax(h, q):
            def body(j, carry):
                b = j // (section // wide)
                c = j % (section // wide)
                at = pl.ds(pl.multiple_of(c * wide, wide), wide)
                left = L[h, b]
                power = jnp.dot(left, RP[:, at], preferred_element_type=F32)
                shape = jnp.dot(left, RS[:, at], preferred_element_type=F32)
                S[h, q, b, :, at] = (1.0 - relax_rate) * M[h, q, b, :, at] + jnp.exp2(power) * shape
                return carry

            lax.fori_loop(0, blocks * (section // wide), body, 0)

        def fill_edge(h):
            inner = kind[1 - h : 2 - h, :] == 1

            for b in range(blocks):
                for t in range(tiles):
                    at = slice(t * LANES, (t + 1) * LANES)
                    S[h, G - 1, b, :, at] = jnp.where(
                        inner[:, at], INF[h, b], S[h, G, b, :, at]
                    )

        def advance_ghost(h, q, step):
            transport([h], q, 1)
            load_coefficients(CG[step, h, :, (G - 1 - q) * section : (G - q) * section])
            relax(h, q)

        def ghost_coefficients(step, h):
            planes = STEPS - 1 - step
            if h == 1:
                parts = [depth - 1 - k for k in range(planes)]
            else:
                parts = list(range(planes))
            return [
                pltpu.make_async_remote_copy(
                    src_ref=CO.at[step, :, columns(x)],
                    dst_ref=CG.at[step, h, :, columns(k)],
                    send_sem=gs_sem.at[step, h, k],
                    recv_sem=gr_sem.at[step, h, k],
                    device_id={"gx": down[h]},
                    device_id_type=MESH,
                )
                for k, x in enumerate(parts)
            ]

        own = pl.ds(pl.multiple_of(me * piece, piece), piece)
        stores = []
        for step in range(STEPS):
            last = step + 1 == STEPS
            if step == 0:
                for copy in loads.values():
                    copy.wait()
            transport([0, 1], G + 1, depth - 1)
            for x in range(depth):
                total = None
                for h in range(2):
                    q = x + G if h == 1 else depth - 1 + G - x
                    if q > G:
                        term = moments(h, q)
                        total = term if total is None else [a + b for a, b in zip(total, term)]
                for c, value in enumerate(total):
                    start = x * section + c * wide
                    PART[step, :, start : start + wide] = value

            for h in range(2):
                @pl.when(has_up[h])
                def _(h=h):
                    halo(h, step).wait_recv()
            finish_halo_send(step)
            if not last:
                start_halo(step + 1)
            for h in range(2):
                @pl.when(has_up[h])
                def _(h=h):
                    if step > 0:
                        if step == 1:
                            for copy in ghost_coefficients(0, h):
                                copy.wait_recv()
                        elif step - 1 < STEPS - 1:
                            for copy in ghost_coefficients(step - 1, h):
                                copy.wait_recv()
                        for level in range(step):
                            advance_ghost(h, G - step + level, level)

                @pl.when(jnp.logical_not(has_up[h]))
                def _(h=h):
                    fill_edge(h)

            transport([0, 1], G, 1)
            for h in range(2):
                x = plane_of(h, G)
                for c, value in enumerate(moments(h, G)):
                    at = slice(x * section + c * wide, x * section + (c + 1) * wide)
                    PART[step, :, at] = PART[step, :, at] + value

            sends = []
            for d in range(1, n_vel):
                to = lax.rem(me + d, n_vel)
                copy = pltpu.make_async_remote_copy(
                    src_ref=PART.at[step, :, pl.ds(pl.multiple_of(to * piece, piece), piece)],
                    dst_ref=GOT.at[step, d],
                    send_sem=ps_sem.at[step, d],
                    recv_sem=pr_sem.at[step, d],
                    device_id={"vel": to},
                    device_id_type=MESH,
                )
                copy.start()
                sends.append(copy)
            total = PART[step, :, own]
            for d in range(1, n_vel):
                sends[d - 1].wait_recv()
                total = total + GOT[step, d]
            CO[step, :, own] = shakhov_rows(total)
            gathers = []
            for d in range(1, n_vel):
                to = lax.rem(me + d, n_vel)
                copy = pltpu.make_async_remote_copy(
                    src_ref=CO.at[step, :, own],
                    dst_ref=CO.at[step, :, own],
                    send_sem=cs_sem.at[step, d],
                    recv_sem=cr_sem.at[step, d],
                    device_id={"vel": to},
                    device_id_type=MESH,
                )
                copy.start()
                gathers.append(copy)
            for copy in gathers:
                copy.wait_recv()
            if not last:
                for h in range(2):
                    @pl.when(has_down[h])
                    def _(h=h):
                        for copy in ghost_coefficients(step, h):
                            copy.start()
            for x in range(depth):
                load_coefficients(CO[step, :, x * section : (x + 1) * section])
                for h in range(2):
                    q = x + G if h == 1 else depth - 1 + G - x
                    relax(h, q)
                    if last:
                        copy = pltpu.make_async_copy(
                            S.at[h, q], out.at[:, h, :, columns(x)], out_sem.at[h, x]
                        )
                        copy.start()
                        stores.append(copy)
            for copy in sends + gathers:
                copy.wait_send()
            if not last:
                for h in range(2):
                    @pl.when(has_down[h])
                    def _(h=h):
                        for copy in ghost_coefficients(step, h):
                            copy.wait_send()
        for copy in stores:
            copy.wait()

    dma = pltpu.SemaphoreType.DMA
    scratch = [
        pltpu.VMEM((2, Q, blocks, half, section), F32),
        pltpu.VMEM((2, Q, blocks, half, section), F32),
        pltpu.VMEM((2, Q, 8, section), F32),
        pltpu.VMEM((STEPS, FEATURES, cells), F32),
        pltpu.VMEM((STEPS, n_vel, FEATURES, piece), F32),
        pltpu.VMEM((STEPS, COEFS, cells), F32),
        pltpu.VMEM((STEPS, 2, COEFS, (STEPS - 1) * section), F32),
        pltpu.VMEM((2, FEATURES, blocks * half), BF16),
        pltpu.VMEM((2, blocks, half, FEATURES * TERMS), BF16),
        pltpu.VMEM((FEATURES * TERMS, section), BF16),
        pltpu.VMEM((FEATURES * TERMS, section), BF16),
        pltpu.VMEM((2, blocks, half, half), F32),
        dma((2, depth)),
        dma((2, depth)),
        dma((2, STEPS)),
        dma((2, STEPS)),
        dma((STEPS, n_vel)),
        dma((STEPS, n_vel)),
        dma((STEPS, n_vel)),
        dma((STEPS, n_vel)),
        dma((STEPS, 2, STEPS)),
        dma((STEPS, 2, STEPS)),
    ]
    return kernel, scratch


def solution(mesh):
    n_vel = mesh.shape["vel"]
    n_gx = mesh.shape["gx"]

    def per_device(distribution, wall_mask, boundary_kind, inflow):
        rows, cells = distribution.shape
        section = wall_mask.shape[1]
        half = VS * VS // 2
        blocks = rows // (2 * half)
        depth = cells // section
        kernel, scratch = make_kernel(n_vel, n_gx, blocks, half, depth, section)
        vmem = pl.BlockSpec(memory_space=pltpu.VMEM)
        out = pl.pallas_call(
            kernel,
            out_shape=jax.ShapeDtypeStruct((blocks, 2, half, cells), F32),
            in_specs=[pl.BlockSpec(memory_space=pl.ANY), vmem, vmem, vmem],
            out_specs=pl.BlockSpec(memory_space=pl.ANY),
            scratch_shapes=scratch,
            compiler_params=pltpu.CompilerParams(
                collective_id=0, has_side_effects=True, vmem_limit_bytes=48 * 1024 * 1024
            ),
        )(
            distribution.reshape(blocks, 2, half, cells),
            wall_mask,
            boundary_kind,
            inflow.reshape(2 * blocks, half),
        )
        return out.reshape(rows, cells)

    placed = (P("vel", "gx"), P(), P(), P("vel"))
    return jax.shard_map(
        per_device, mesh=mesh, in_specs=placed, out_specs=P("vel", "gx"), check_vma=False
    )
```

```python
import math

import jax
import jax.numpy as jnp
from jax import lax
from jax.experimental import pallas as pl
from jax.experimental.pallas import tpu as pltpu
from jax.sharding import PartitionSpec as P

VS = 16
NY = 16
NZ = 32
STEPS = 3
LANES = 128
FEATURES = 16
TERMS = 3
COEFS = 24

vel_limit = 4.5
time_step = 0.075
relax_rate = 0.6
viscous_thermal_ratio = 0.6666667
spacing = 2.0 * vel_limit / VS
unit = spacing / 2.0
MESH = pl.DeviceIdType.MESH
F32 = jnp.float32
BF16 = jnp.bfloat16


def features(index, cx, cy, cz):
    energy = cx * cx + cy * cy + cz * cz

    def high(value):
        return jnp.floor(value * (1.0 / 64.0)) * 64.0

    cubes = [energy * cx, energy * cy, energy * cz]
    rows = [jnp.ones_like(cx), cx, cy, cz, cx * cx, cy * cy, cz * cz, cx * cy, cx * cz, cy * cz]
    rows += [high(c) for c in cubes]
    rows += [c - high(c) for c in cubes]
    out = rows[0]
    for k in range(1, FEATURES):
        out = jnp.where(index == k, rows[k], out)
    return out


def shakhov_rows(moments):
    weight = spacing**3
    degree = [0, 1, 1, 1, 2, 2, 2, 2, 2, 2, 3, 3, 3]
    m = [moments[k : k + 1] for k in range(FEATURES)]
    m = m[:10] + [m[10 + a] + m[13 + a] for a in range(3)]
    m = [row * (weight * unit**d) for row, d in zip(m, degree)]
    n = m[0]
    inv_n = 1.0 / n
    u = [m[1] * inv_n, m[2] * inv_n, m[3] * inv_n]
    xx, yy, zz, xy, xz, yz = m[4:10]
    uu = u[0] * u[0] + u[1] * u[1] + u[2] * u[2]
    tr = xx + yy + zz
    temp = (tr * inv_n - uu) / 3.0
    press = [
        xx * u[0] + xy * u[1] + xz * u[2],
        xy * u[0] + yy * u[1] + yz * u[2],
        xz * u[0] + yz * u[1] + zz * u[2],
    ]
    q = [0.5 * (m[10 + a] - 2.0 * press[a] - u[a] * tr + 2.0 * n * uu * u[a]) for a in range(3)]
    inv_t = 1.0 / temp
    kappa = (1.0 - viscous_thermal_ratio) / (5.0 * n * temp * temp)
    s = kappa * inv_t
    uq = u[0] * q[0] + u[1] * q[1] + u[2] * q[2]
    first = jnp.log(n) - 1.5 * jnp.log(2.0 * math.pi * temp) - uu * (0.5 * inv_t)
    quad = -0.5 * inv_t
    expo = [first, u[0] * inv_t, u[1] * inv_t, u[2] * inv_t, quad, quad, quad]
    expo = [row * (math.log2(math.e) * unit**d) for row, d in zip(expo, [0, 1, 1, 1, 2, 2, 2])]
    poly = [1.0 - s * uq * uu + 5.0 * kappa * uq]
    poly += [s * (q[a] * uu + 2.0 * uq * u[a]) - 5.0 * kappa * q[a] for a in range(3)]
    poly += [-2.0 * s * q[a] * u[a] - s * uq for a in range(3)]
    poly += [-2.0 * s * (q[a] * u[b] + q[b] * u[a]) for a, b in ((0, 1), (0, 2), (1, 2))]
    poly += [s * q[a] for a in range(3)]
    poly = [row * (relax_rate * unit**d) for row, d in zip(poly, degree)]
    poly += poly[10:13]
    return jnp.concatenate(expo + [jnp.zeros_like(n)] + poly, axis=0)


def make_kernel(n_vel, n_gx, blocks, half, depth, section, planes):
    G = STEPS
    Q = depth + G
    cells = depth * section
    piece = cells // n_vel
    tiles = section // LANES
    wide = 2 * LANES
    zh_rows = VS // 2

    def plane_of(h, q):
        return q - G if h == 1 else depth - 1 + G - q

    def kernel(
        dist, wall_in, kind_in, inflow_in, out,
        S, M, H, PART, GOT, CO, CG, PHI, L, RP, RS, INF, wall, kind, inflow, sm_sem,
        in_sem, out_sem, hs_sem, hr_sem, ps_sem, pr_sem, cs_sem, cr_sem, gs_sem, gr_sem,
    ):
        me = lax.axis_index("vel")
        pos = lax.axis_index("gx")
        has_left = pos > 0
        has_right = pos < n_gx - 1
        has_up = [has_right, has_left]
        has_down = [has_left, has_right]
        up = [pos + 1, pos - 1]
        down = [pos - 1, pos + 1]

        def columns(x):
            return pl.ds(x * section, section)

        loads = {}
        for q in range(Q - 1, G - 1, -1):
            for h in range(2):
                copy = pltpu.make_async_copy(
                    dist.at[:, h, :, columns(plane_of(h, q))], S.at[h, q], in_sem.at[h, q - G]
                )
                copy.start()
                loads[h, q] = copy

        small = []
        for k, (src, dst) in enumerate(((wall_in, wall), (kind_in, kind), (inflow_in, inflow))):
            copy = pltpu.make_async_copy(src, dst, sm_sem.at[k])
            copy.start()
            small.append(copy)

        barrier = pltpu.get_barrier_semaphore()
        for d in range(1, n_vel):
            pl.semaphore_signal(
                barrier, inc=1, device_id={"vel": lax.rem(me + d, n_vel)}, device_id_type=MESH
            )
        for h in range(2):
            @pl.when(has_down[h])
            def _(h=h):
                pl.semaphore_signal(barrier, inc=1, device_id={"gx": down[h]}, device_id_type=MESH)
        met = n_vel - 1 + has_left.astype(jnp.int32) + has_right.astype(jnp.int32)
        pl.semaphore_wait(barrier, met)

        def halo(h, k):
            x = depth - 1 - k if h == 1 else k
            return pltpu.make_async_remote_copy(
                src_ref=dist.at[:, h, :, columns(x)],
                dst_ref=S.at[h, G - 1 - k],
                send_sem=hs_sem.at[h, k],
                recv_sem=hr_sem.at[h, k],
                device_id={"gx": down[h]},
                device_id_type=MESH,
            )

        def start_halo(k):
            for h in range(2):
                @pl.when(has_down[h])
                def _(h=h):
                    halo(h, k).start()

        def finish_halo_send(k):
            for h in range(2):
                @pl.when(has_down[h])
                def _(h=h):
                    halo(h, k).wait_send()

        start_halo(0)

        for copy in small:
            copy.wait()

        first_iy = me * blocks
        lane = lax.broadcasted_iota(jnp.int32, (1, section), 1)
        y_at = lane // NZ
        z_at = lane % NZ
        vy_up = first_iy >= VS // 2
        n_planes = wall.shape[0]

        def openness(x):
            at = pos * depth + x
            row = wall[pl.ds(jnp.clip(at, 0, n_planes - 1), 1), :]
            inside = jnp.logical_and(at >= 0, at < n_planes)
            return jnp.where(inside, (1 - row).astype(F32), 1.0)

        for h in range(2):
            way = 1 if h == 1 else -1
            for q in range(1, Q):
                x = plane_of(h, q)
                o = openness(x)
                x_in = o * openness(x - way)
                x_out = o * openness(x + way)
                y_hi = jnp.where(y_at < NY - 1, o * pltpu.roll(o, section - NZ, 1), 0.0)
                y_lo = jnp.where(y_at > 0, o * pltpu.roll(o, NZ, 1), 0.0)
                z_hi = jnp.where(z_at < NZ - 1, o * pltpu.roll(o, section - 1, 1), 0.0)
                z_lo = jnp.where(z_at > 0, o * pltpu.roll(o, 1, 1), 0.0)
                y_in = jnp.where(vy_up, y_lo, y_hi)
                y_out = jnp.where(vy_up, y_hi, y_lo)
                rows = [x_in, x_out, y_in, y_out, z_hi, z_lo, z_lo, z_hi]
                H[h, q] = jnp.concatenate([r * time_step for r in rows], axis=0)

        for h in range(2):
            sign = 1.0 if h == 1 else -1.0
            shape = (FEATURES, blocks * half)
            r = lax.broadcasted_iota(jnp.int32, shape, 1)
            index = lax.broadcasted_iota(jnp.int32, shape, 0)
            cx = sign * (2 * ((r % half) // VS) + 1).astype(F32)
            cz = (2 * (r % VS) - (VS - 1)).astype(F32)
            cy = (2 * (first_iy + r // half) - (VS - 1)).astype(F32)
            PHI[h] = features(index, cx, cy, cz).astype(BF16)
            shape = (half, FEATURES * TERMS)
            r = lax.broadcasted_iota(jnp.int32, shape, 0)
            index = lax.broadcasted_iota(jnp.int32, shape, 1) % FEATURES
            cx = sign * (2 * (r // VS) + 1).astype(F32)
            cz = (2 * (r % VS) - (VS - 1)).astype(F32)
            for b in range(blocks):
                cy = jnp.full(shape, 2 * (first_iy + b) - (VS - 1), jnp.int32).astype(F32)
                L[h, b] = features(index, cx, cy, cz).astype(BF16)
                row = inflow[2 * b + h : 2 * b + h + 1, :]
                INF[h, b] = jnp.broadcast_to(row, (half, half)).T

        lane_t = lax.broadcasted_iota(jnp.int32, (zh_rows, LANES), 1)
        sub = lax.broadcasted_iota(jnp.int32, (zh_rows, LANES), 0).astype(F32)
        y_take = jnp.where(vy_up, LANES - NZ, 0)
        from_next = jnp.logical_and(lane_t >= y_take, lane_t < y_take + NZ)
        y_shift = jnp.where(vy_up, NZ, LANES - NZ)
        t_step = jnp.where(vy_up, tiles - 1, 1)

        def transport(h_list, q0, nq):
            nh = len(h_list)

            def body(j, carry):
                b = lax.rem(j, blocks)
                outer = lax.div(j, blocks)
                h = lax.rem(outer, nh) if nh == 2 else h_list[0]
                q = q0 + lax.div(outer, nh)
                speed_y = jnp.abs(-vel_limit + ((first_iy + b).astype(F32) + 0.5) * spacing)
                for t in range(tiles):
                    at = slice(t * LANES, (t + 1) * LANES)
                    t_next = lax.rem(t + t_step, tiles)
                    at_next = pl.ds(pl.multiple_of(t_next * LANES, LANES), LANES)

                    def face(k):
                        return jnp.broadcast_to(H[h, q, k : k + 1, at], (zh_rows, LANES))

                    x_in, x_out = face(0), face(1)
                    y_in = face(2) * speed_y
                    y_keep = 1.0 - face(3) * speed_y
                    for zh in range(2):
                        if zh == 0:
                            speed_z = vel_limit - (sub + 0.5) * spacing
                        else:
                            speed_z = (sub + 0.5) * spacing
                        z_in = face(4 + 2 * zh) * speed_z
                        keep = y_keep - face(5 + 2 * zh) * speed_z
                        for i in range(half // VS):
                            rows = pl.ds(i * VS + zh * zh_rows, zh_rows)
                            speed_x = (i + 0.5) * spacing
                            f = S[h, q, b, rows, at]
                            before = S[h, q - 1, b, rows, at]
                            beside = S[h, q, b, rows, at_next]
                            f_y = pltpu.roll(jnp.where(from_next, beside, f), y_shift, 1)
                            f_z = pltpu.roll(f, 1 if zh == 1 else LANES - 1, 1)
                            moved = f * (keep - x_out * speed_x) + before * (x_in * speed_x)
                            moved = moved + (f_y * y_in + f_z * z_in)
                            M[h, q, b, rows, at] = moved
                return carry

            lax.fori_loop(0, nh * nq * blocks, body, 0)

        def moments(h, q):
            halves = []
            for c in range(section // wide):
                value = M[h, q, :, :, c * wide : (c + 1) * wide].reshape(blocks * half, wide)
                hi = value.astype(BF16)
                lo = (value - hi.astype(F32)).astype(BF16)
                phi = PHI[h]
                halves.append(
                    jnp.dot(phi, hi, preferred_element_type=F32)
                    + jnp.dot(phi, lo, preferred_element_type=F32)
                )
            return halves

        def load_coefficients(rows, slot):
            terms = []
            rest = rows
            for j in range(TERMS):
                term = rest.astype(BF16)
                terms.append(term)
                rest = rest - term.astype(F32)
            for j in range(TERMS):
                at = slice(j * FEATURES, (j + 1) * FEATURES)
                RP[slot, at, :] = jnp.concatenate(
                    [terms[j][0:8], jnp.zeros((8, section), BF16)], axis=0
                )
                RS[slot, at, :] = terms[j][8:COEFS]

        def relax(h, q, slot):
            for c in range(section // wide):
                at = slice(c * wide, (c + 1) * wide)
                left = L[h].reshape(blocks * half, FEATURES * TERMS)
                power = jnp.dot(left, RP[slot, :, at], preferred_element_type=F32)
                shape = jnp.dot(left, RS[slot, :, at], preferred_element_type=F32)
                fresh = (jnp.exp2(power) * shape).reshape(blocks, half, wide)
                S[h, q, :, :, at] = (1.0 - relax_rate) * M[h, q, :, :, at] + fresh

        def fill_edge(h):
            inner = kind[1 - h : 2 - h, :] == 1

            for b in range(blocks):
                for t in range(tiles):
                    at = slice(t * LANES, (t + 1) * LANES)
                    S[h, G - 1, b, :, at] = jnp.where(
                        inner[:, at], INF[h, b], S[h, G, b, :, at]
                    )

        def advance_ghost(h, q, step):
            transport([h], q, 1)
            load_coefficients(CG[step, h, :, (G - 1 - q) * section : (G - q) * section], 0)
            relax(h, q, 0)

        def ghost_coefficients(step, h):
            ghosts = STEPS - 1 - step
            if h == 1:
                parts = [depth - 1 - k for k in range(ghosts)]
            else:
                parts = list(range(ghosts))
            return [
                pltpu.make_async_remote_copy(
                    src_ref=CO.at[step, :, columns(x)],
                    dst_ref=CG.at[step, h, :, columns(k)],
                    send_sem=gs_sem.at[step, h, k],
                    recv_sem=gr_sem.at[step, h, k],
                    device_id={"gx": down[h]},
                    device_id_type=MESH,
                )
                for k, x in enumerate(parts)
            ]

        own = pl.ds(pl.multiple_of(me * piece, piece), piece)
        stores = []
        for step in range(STEPS):
            last = step + 1 == STEPS
            if step == 0:
                for copy in loads.values():
                    copy.wait()
            transport([0, 1], G + 1, depth - 1)
            for x in range(depth):
                total = None
                for h in range(2):
                    q = x + G if h == 1 else depth - 1 + G - x
                    if q > G:
                        term = moments(h, q)
                        total = term if total is None else [a + b for a, b in zip(total, term)]
                for c, value in enumerate(total):
                    start = x * section + c * wide
                    PART[step, :, start : start + wide] = value

            for h in range(2):
                @pl.when(has_up[h])
                def _(h=h):
                    halo(h, step).wait_recv()
            finish_halo_send(step)
            if not last:
                start_halo(step + 1)
            for h in range(2):
                @pl.when(has_up[h])
                def _(h=h):
                    if step > 0:
                        if step == 1:
                            for copy in ghost_coefficients(0, h):
                                copy.wait_recv()
                        elif step - 1 < STEPS - 1:
                            for copy in ghost_coefficients(step - 1, h):
                                copy.wait_recv()
                        for level in range(step):
                            advance_ghost(h, G - step + level, level)

                @pl.when(jnp.logical_not(has_up[h]))
                def _(h=h):
                    fill_edge(h)

            transport([0, 1], G, 1)
            for h in range(2):
                x = plane_of(h, G)
                for c, value in enumerate(moments(h, G)):
                    at = slice(x * section + c * wide, x * section + (c + 1) * wide)
                    PART[step, :, at] = PART[step, :, at] + value

            sends = []
            for d in range(1, n_vel):
                to = lax.rem(me + d, n_vel)
                copy = pltpu.make_async_remote_copy(
                    src_ref=PART.at[step, :, pl.ds(pl.multiple_of(to * piece, piece), piece)],
                    dst_ref=GOT.at[step, d],
                    send_sem=ps_sem.at[step, d],
                    recv_sem=pr_sem.at[step, d],
                    device_id={"vel": to},
                    device_id_type=MESH,
                )
                copy.start()
                sends.append(copy)
            total = PART[step, :, own]
            for d in range(1, n_vel):
                sends[d - 1].wait_recv()
                total = total + GOT[step, d]
            CO[step, :, own] = shakhov_rows(total)
            gathers = []
            for d in range(1, n_vel):
                to = lax.rem(me + d, n_vel)
                copy = pltpu.make_async_remote_copy(
                    src_ref=CO.at[step, :, own],
                    dst_ref=CO.at[step, :, own],
                    send_sem=cs_sem.at[step, d],
                    recv_sem=cr_sem.at[step, d],
                    device_id={"vel": to},
                    device_id_type=MESH,
                )
                copy.start()
                gathers.append(copy)
            for copy in gathers:
                copy.wait_recv()
            if not last:
                for h in range(2):
                    @pl.when(has_down[h])
                    def _(h=h):
                        for copy in ghost_coefficients(step, h):
                            copy.start()
            for x in range(depth):
                load_coefficients(CO[step, :, x * section : (x + 1) * section], x % 2)
                for h in range(2):
                    q = x + G if h == 1 else depth - 1 + G - x
                    relax(h, q, x % 2)
                    if last:
                        copy = pltpu.make_async_copy(
                            S.at[h, q], out.at[:, h, :, columns(x)], out_sem.at[h, x]
                        )
                        copy.start()
                        stores.append(copy)
            for copy in sends + gathers:
                copy.wait_send()
            if not last:
                for h in range(2):
                    @pl.when(has_down[h])
                    def _(h=h):
                        for copy in ghost_coefficients(step, h):
                            copy.wait_send()
        for copy in stores:
            copy.wait()

    dma = pltpu.SemaphoreType.DMA
    scratch = [
        pltpu.VMEM((2, Q, blocks, half, section), F32),
        pltpu.VMEM((2, Q, blocks, half, section), F32),
        pltpu.VMEM((2, Q, 8, section), F32),
        pltpu.VMEM((STEPS, FEATURES, cells), F32),
        pltpu.VMEM((STEPS, n_vel, FEATURES, piece), F32),
        pltpu.VMEM((STEPS, COEFS, cells), F32),
        pltpu.VMEM((STEPS, 2, COEFS, (STEPS - 1) * section), F32),
        pltpu.VMEM((2, FEATURES, blocks * half), BF16),
        pltpu.VMEM((2, blocks, half, FEATURES * TERMS), BF16),
        pltpu.VMEM((2, FEATURES * TERMS, section), BF16),
        pltpu.VMEM((2, FEATURES * TERMS, section), BF16),
        pltpu.VMEM((2, blocks, half, half), F32),
        pltpu.VMEM((planes, section), jnp.int32),
        pltpu.VMEM((2, section), jnp.int32),
        pltpu.VMEM((2 * blocks, half), F32),
        dma((3,)),
        dma((2, depth)),
        dma((2, depth)),
        dma((2, STEPS)),
        dma((2, STEPS)),
        dma((STEPS, n_vel)),
        dma((STEPS, n_vel)),
        dma((STEPS, n_vel)),
        dma((STEPS, n_vel)),
        dma((STEPS, 2, STEPS)),
        dma((STEPS, 2, STEPS)),
    ]
    return kernel, scratch


def solution(mesh):
    n_vel = mesh.shape["vel"]
    n_gx = mesh.shape["gx"]

    def per_device(distribution, wall_mask, boundary_kind, inflow):
        rows, cells = distribution.shape
        section = wall_mask.shape[1]
        half = VS * VS // 2
        blocks = rows // (2 * half)
        depth = cells // section
        kernel, scratch = make_kernel(n_vel, n_gx, blocks, half, depth, section, wall_mask.shape[0])
        whole = pl.BlockSpec(memory_space=pl.ANY)
        out = pl.pallas_call(
            kernel,
            out_shape=jax.ShapeDtypeStruct((blocks, 2, half, cells), F32),
            in_specs=[whole] * 4,
            out_specs=whole,
            scratch_shapes=scratch,
            compiler_params=pltpu.CompilerParams(
                collective_id=0, has_side_effects=True, vmem_limit_bytes=48 * 1024 * 1024
            ),
        )(
            distribution.reshape(blocks, 2, half, cells),
            wall_mask,
            boundary_kind,
            inflow.reshape(2 * blocks, half),
        )
        return out.reshape(rows, cells)

    placed = (P("vel", "gx"), P(), P(), P("vel"))
    return jax.shard_map(
        per_device, mesh=mesh, in_specs=placed, out_specs=P("vel", "gx"), check_vma=False
    )
```

```python
import math

import jax
import jax.numpy as jnp
from jax import lax
from jax.experimental import pallas as pl
from jax.experimental.pallas import tpu as pltpu
from jax.sharding import PartitionSpec as P

VS = 16
NY = 16
NZ = 32
STEPS = 3
LANES = 128
FEATURES = 16
TERMS = 3
COEFS = 24

vel_limit = 4.5
time_step = 0.075
relax_rate = 0.6
viscous_thermal_ratio = 0.6666667
spacing = 2.0 * vel_limit / VS
unit = spacing / 2.0
MESH = pl.DeviceIdType.MESH
F32 = jnp.float32
BF16 = jnp.bfloat16


def features(index, cx, cy, cz):
    energy = cx * cx + cy * cy + cz * cz

    def high(value):
        return jnp.floor(value * (1.0 / 64.0)) * 64.0

    cubes = [energy * cx, energy * cy, energy * cz]
    rows = [jnp.ones_like(cx), cx, cy, cz, cx * cx, cy * cy, cz * cz, cx * cy, cx * cz, cy * cz]
    rows += [high(c) for c in cubes]
    rows += [c - high(c) for c in cubes]
    out = rows[0]
    for k in range(1, FEATURES):
        out = jnp.where(index == k, rows[k], out)
    return out


def shakhov_rows(moments):
    weight = spacing**3
    degree = [0, 1, 1, 1, 2, 2, 2, 2, 2, 2, 3, 3, 3]
    m = [moments[k : k + 1] for k in range(FEATURES)]
    m = m[:10] + [m[10 + a] + m[13 + a] for a in range(3)]
    m = [row * (weight * unit**d) for row, d in zip(m, degree)]
    n = m[0]
    inv_n = 1.0 / n
    u = [m[1] * inv_n, m[2] * inv_n, m[3] * inv_n]
    xx, yy, zz, xy, xz, yz = m[4:10]
    uu = u[0] * u[0] + u[1] * u[1] + u[2] * u[2]
    tr = xx + yy + zz
    temp = (tr * inv_n - uu) / 3.0
    press = [
        xx * u[0] + xy * u[1] + xz * u[2],
        xy * u[0] + yy * u[1] + yz * u[2],
        xz * u[0] + yz * u[1] + zz * u[2],
    ]
    q = [0.5 * (m[10 + a] - 2.0 * press[a] - u[a] * tr + 2.0 * n * uu * u[a]) for a in range(3)]
    inv_t = 1.0 / temp
    kappa = (1.0 - viscous_thermal_ratio) / (5.0 * n * temp * temp)
    s = kappa * inv_t
    uq = u[0] * q[0] + u[1] * q[1] + u[2] * q[2]
    first = jnp.log(n) - 1.5 * jnp.log(2.0 * math.pi * temp) - uu * (0.5 * inv_t)
    quad = -0.5 * inv_t
    expo = [first, u[0] * inv_t, u[1] * inv_t, u[2] * inv_t, quad, quad, quad]
    expo = [row * (math.log2(math.e) * unit**d) for row, d in zip(expo, [0, 1, 1, 1, 2, 2, 2])]
    poly = [1.0 - s * uq * uu + 5.0 * kappa * uq]
    poly += [s * (q[a] * uu + 2.0 * uq * u[a]) - 5.0 * kappa * q[a] for a in range(3)]
    poly += [-2.0 * s * q[a] * u[a] - s * uq for a in range(3)]
    poly += [-2.0 * s * (q[a] * u[b] + q[b] * u[a]) for a, b in ((0, 1), (0, 2), (1, 2))]
    poly += [s * q[a] for a in range(3)]
    poly = [row * (relax_rate * unit**d) for row, d in zip(poly, degree)]
    poly += poly[10:13]
    return jnp.concatenate(expo + [jnp.zeros_like(n)] + poly, axis=0)


def make_kernel(n_vel, n_gx, blocks, half, depth, section, planes):
    G = STEPS
    Q = depth + G
    cells = depth * section
    groups = [list(range(1, depth - 1)), [0, depth - 1]]
    if len(groups[0]) != len(groups[1]) or cells // 2 % (n_vel * LANES):
        groups = [list(range(depth))]
    order = [x for group in groups for x in group]
    span = cells // len(groups)
    piece = span // n_vel
    tiles = section // LANES
    wide = 2 * LANES
    zh_rows = VS // 2

    def plane_of(h, q):
        return q - G if h == 1 else depth - 1 + G - q

    def kernel(
        dist, wall_in, kind_in, inflow_in, out,
        S, M, H, PART, GOT, CO, CG, PHI, L, RP, RS, INF, wall, kind, inflow, sm_sem,
        in_sem, out_sem, hs_sem, hr_sem, ps_sem, pr_sem, cs_sem, cr_sem, gs_sem, gr_sem,
    ):
        me = lax.axis_index("vel")
        pos = lax.axis_index("gx")
        has_left = pos > 0
        has_right = pos < n_gx - 1
        has_up = [has_right, has_left]
        has_down = [has_left, has_right]
        up = [pos + 1, pos - 1]
        down = [pos - 1, pos + 1]

        def columns(x):
            return pl.ds(x * section, section)

        def place(x):
            return pl.ds(order.index(x) * section, section)

        def q_of(h, x):
            return x + G if h == 1 else depth - 1 + G - x

        loads = {}
        for q in range(Q - 1, G - 1, -1):
            for h in range(2):
                copy = pltpu.make_async_copy(
                    dist.at[:, h, :, columns(plane_of(h, q))], S.at[h, q], in_sem.at[h, q - G]
                )
                copy.start()
                loads[h, q] = copy

        small = []
        for k, (src, dst) in enumerate(((wall_in, wall), (kind_in, kind), (inflow_in, inflow))):
            copy = pltpu.make_async_copy(src, dst, sm_sem.at[k])
            copy.start()
            small.append(copy)

        barrier = pltpu.get_barrier_semaphore()
        for d in range(1, n_vel):
            pl.semaphore_signal(
                barrier, inc=1, device_id={"vel": lax.rem(me + d, n_vel)}, device_id_type=MESH
            )
        for h in range(2):
            @pl.when(has_down[h])
            def _(h=h):
                pl.semaphore_signal(barrier, inc=1, device_id={"gx": down[h]}, device_id_type=MESH)
        met = n_vel - 1 + has_left.astype(jnp.int32) + has_right.astype(jnp.int32)
        pl.semaphore_wait(barrier, met)

        def halo(h, k):
            x = depth - 1 - k if h == 1 else k
            return pltpu.make_async_remote_copy(
                src_ref=dist.at[:, h, :, columns(x)],
                dst_ref=S.at[h, G - 1 - k],
                send_sem=hs_sem.at[h, k],
                recv_sem=hr_sem.at[h, k],
                device_id={"gx": down[h]},
                device_id_type=MESH,
            )

        def start_halo(k):
            for h in range(2):
                @pl.when(has_down[h])
                def _(h=h):
                    halo(h, k).start()

        def finish_halo_send(k):
            for h in range(2):
                @pl.when(has_down[h])
                def _(h=h):
                    halo(h, k).wait_send()

        start_halo(0)

        for copy in small:
            copy.wait()

        first_iy = me * blocks
        lane = lax.broadcasted_iota(jnp.int32, (1, section), 1)
        y_at = lane // NZ
        z_at = lane % NZ
        vy_up = first_iy >= VS // 2
        n_planes = wall.shape[0]

        def openness(x):
            at = pos * depth + x
            row = wall[pl.ds(jnp.clip(at, 0, n_planes - 1), 1), :]
            inside = jnp.logical_and(at >= 0, at < n_planes)
            return jnp.where(inside, (1 - row).astype(F32), 1.0)

        for h in range(2):
            way = 1 if h == 1 else -1
            for q in range(1, Q):
                x = plane_of(h, q)
                o = openness(x)
                x_in = o * openness(x - way)
                x_out = o * openness(x + way)
                y_hi = jnp.where(y_at < NY - 1, o * pltpu.roll(o, section - NZ, 1), 0.0)
                y_lo = jnp.where(y_at > 0, o * pltpu.roll(o, NZ, 1), 0.0)
                z_hi = jnp.where(z_at < NZ - 1, o * pltpu.roll(o, section - 1, 1), 0.0)
                z_lo = jnp.where(z_at > 0, o * pltpu.roll(o, 1, 1), 0.0)
                y_in = jnp.where(vy_up, y_lo, y_hi)
                y_out = jnp.where(vy_up, y_hi, y_lo)
                rows = [x_in, x_out, y_in, y_out, z_hi, z_lo, z_lo, z_hi]
                H[h, q] = jnp.concatenate([r * time_step for r in rows], axis=0)

        for h in range(2):
            sign = 1.0 if h == 1 else -1.0
            shape = (FEATURES, blocks * half)
            r = lax.broadcasted_iota(jnp.int32, shape, 1)
            index = lax.broadcasted_iota(jnp.int32, shape, 0)
            cx = sign * (2 * ((r % half) // VS) + 1).astype(F32)
            cz = (2 * (r % VS) - (VS - 1)).astype(F32)
            cy = (2 * (first_iy + r // half) - (VS - 1)).astype(F32)
            PHI[h] = features(index, cx, cy, cz).astype(BF16)
            shape = (half, FEATURES * TERMS)
            r = lax.broadcasted_iota(jnp.int32, shape, 0)
            index = lax.broadcasted_iota(jnp.int32, shape, 1) % FEATURES
            cx = sign * (2 * (r // VS) + 1).astype(F32)
            cz = (2 * (r % VS) - (VS - 1)).astype(F32)
            for b in range(blocks):
                cy = jnp.full(shape, 2 * (first_iy + b) - (VS - 1), jnp.int32).astype(F32)
                L[h, b] = features(index, cx, cy, cz).astype(BF16)
                row = inflow[2 * b + h : 2 * b + h + 1, :]
                INF[h, b] = jnp.broadcast_to(row, (half, half)).T

        lane_t = lax.broadcasted_iota(jnp.int32, (zh_rows, LANES), 1)
        sub = lax.broadcasted_iota(jnp.int32, (zh_rows, LANES), 0).astype(F32)
        y_take = jnp.where(vy_up, LANES - NZ, 0)
        from_next = jnp.logical_and(lane_t >= y_take, lane_t < y_take + NZ)
        y_shift = jnp.where(vy_up, NZ, LANES - NZ)
        t_step = jnp.where(vy_up, tiles - 1, 1)

        def transport(h_list, q0, nq):
            nh = len(h_list)

            def body(j, carry):
                b = lax.rem(j, blocks)
                outer = lax.div(j, blocks)
                h = lax.rem(outer, nh) if nh == 2 else h_list[0]
                q = q0 + lax.div(outer, nh)
                speed_y = jnp.abs(-vel_limit + ((first_iy + b).astype(F32) + 0.5) * spacing)
                for t in range(tiles):
                    at = slice(t * LANES, (t + 1) * LANES)
                    t_next = lax.rem(t + t_step, tiles)
                    at_next = pl.ds(pl.multiple_of(t_next * LANES, LANES), LANES)

                    def face(k):
                        return jnp.broadcast_to(H[h, q, k : k + 1, at], (zh_rows, LANES))

                    x_in, x_out = face(0), face(1)
                    y_in = face(2) * speed_y
                    y_keep = 1.0 - face(3) * speed_y
                    for zh in range(2):
                        if zh == 0:
                            speed_z = vel_limit - (sub + 0.5) * spacing
                        else:
                            speed_z = (sub + 0.5) * spacing
                        z_in = face(4 + 2 * zh) * speed_z
                        keep = y_keep - face(5 + 2 * zh) * speed_z
                        for i in range(half // VS):
                            rows = pl.ds(i * VS + zh * zh_rows, zh_rows)
                            speed_x = (i + 0.5) * spacing
                            f = S[h, q, b, rows, at]
                            before = S[h, q - 1, b, rows, at]
                            beside = S[h, q, b, rows, at_next]
                            f_y = pltpu.roll(jnp.where(from_next, beside, f), y_shift, 1)
                            f_z = pltpu.roll(f, 1 if zh == 1 else LANES - 1, 1)
                            moved = f * (keep - x_out * speed_x) + before * (x_in * speed_x)
                            moved = moved + (f_y * y_in + f_z * z_in)
                            M[h, q, b, rows, at] = moved
                return carry

            lax.fori_loop(0, nh * nq * blocks, body, 0)

        def moments(h, q):
            halves = []
            for c in range(section // wide):
                value = M[h, q, :, :, c * wide : (c + 1) * wide].reshape(blocks * half, wide)
                hi = value.astype(BF16)
                lo = (value - hi.astype(F32)).astype(BF16)
                phi = PHI[h]
                halves.append(
                    jnp.dot(phi, hi, preferred_element_type=F32)
                    + jnp.dot(phi, lo, preferred_element_type=F32)
                )
            return halves

        def load_coefficients(rows, slot):
            terms = []
            rest = rows
            for j in range(TERMS):
                term = rest.astype(BF16)
                terms.append(term)
                rest = rest - term.astype(F32)
            for j in range(TERMS):
                at = slice(j * FEATURES, (j + 1) * FEATURES)
                RP[slot, at, :] = jnp.concatenate(
                    [terms[j][0:8], jnp.zeros((8, section), BF16)], axis=0
                )
                RS[slot, at, :] = terms[j][8:COEFS]

        def relax(h, q, slot):
            for c in range(section // wide):
                at = slice(c * wide, (c + 1) * wide)
                left = L[h].reshape(blocks * half, FEATURES * TERMS)
                power = jnp.dot(left, RP[slot, :, at], preferred_element_type=F32)
                shape = jnp.dot(left, RS[slot, :, at], preferred_element_type=F32)
                fresh = (jnp.exp2(power) * shape).reshape(blocks, half, wide)
                S[h, q, :, :, at] = (1.0 - relax_rate) * M[h, q, :, :, at] + fresh

        def fill_edge(h):
            inner = kind[1 - h : 2 - h, :] == 1

            for b in range(blocks):
                for t in range(tiles):
                    at = slice(t * LANES, (t + 1) * LANES)
                    S[h, G - 1, b, :, at] = jnp.where(
                        inner[:, at], INF[h, b], S[h, G, b, :, at]
                    )

        def advance_ghost(h, q, step):
            transport([h], q, 1)
            load_coefficients(CG[step, h, :, (G - 1 - q) * section : (G - q) * section], 0)
            relax(h, q, 0)

        def ghost_coefficients(step, h):
            ghosts = STEPS - 1 - step
            if h == 1:
                parts = [depth - 1 - k for k in range(ghosts)]
            else:
                parts = list(range(ghosts))
            return [
                pltpu.make_async_remote_copy(
                    src_ref=CO.at[step, :, place(x)],
                    dst_ref=CG.at[step, h, :, columns(k)],
                    send_sem=gs_sem.at[step, h, k],
                    recv_sem=gr_sem.at[step, h, k],
                    device_id={"gx": down[h]},
                    device_id_type=MESH,
                )
                for k, x in enumerate(parts)
            ]

        def share(g, who):
            return pl.ds(pl.multiple_of(g * span + who * piece, piece), piece)

        def store_moments(step, x, values):
            for c, value in enumerate(values):
                start = order.index(x) * section + c * wide
                PART[step, :, start : start + wide] = value

        def add_moments(step, x, values):
            for c, value in enumerate(values):
                start = order.index(x) * section + c * wide
                at = slice(start, start + wide)
                PART[step, :, at] = PART[step, :, at] + value

        def send_moments(step, g):
            copies = []
            for d in range(1, n_vel):
                to = lax.rem(me + d, n_vel)
                copy = pltpu.make_async_remote_copy(
                    src_ref=PART.at[step, :, share(g, to)],
                    dst_ref=GOT.at[step, g, d],
                    send_sem=ps_sem.at[step, g, d],
                    recv_sem=pr_sem.at[step, g, d],
                    device_id={"vel": to},
                    device_id_type=MESH,
                )
                copy.start()
                copies.append(copy)
            return copies

        def send_coefficients(step, g, sends):
            total = PART[step, :, share(g, me)]
            for d in range(1, n_vel):
                sends[d - 1].wait_recv()
                total = total + GOT[step, g, d]
            CO[step, :, share(g, me)] = shakhov_rows(total)
            copies = []
            for d in range(1, n_vel):
                copy = pltpu.make_async_remote_copy(
                    src_ref=CO.at[step, :, share(g, me)],
                    dst_ref=CO.at[step, :, share(g, me)],
                    send_sem=cs_sem.at[step, g, d],
                    recv_sem=cr_sem.at[step, g, d],
                    device_id={"vel": lax.rem(me + d, n_vel)},
                    device_id_type=MESH,
                )
                copy.start()
                copies.append(copy)
            return copies

        def ghost_copies(step, h, g):
            copies = ghost_coefficients(step, h)
            return [
                copy
                for k, copy in enumerate(copies)
                if (depth - 1 - k if h == 1 else k) in groups[g]
            ]

        stores = []

        def relax_group(step, g, gathers):
            for copy in gathers:
                copy.wait_recv()
            for h in range(2):
                forwards = ghost_copies(step, h, g)
                if forwards:
                    @pl.when(has_down[h])
                    def _(forwards=forwards):
                        for copy in forwards:
                            copy.start()
            for n, x in enumerate(groups[g]):
                load_coefficients(CO[step, :, place(x)], n % 2)
                for h in range(2):
                    q = q_of(h, x)
                    relax(h, q, n % 2)
                    if step + 1 == STEPS:
                        copy = pltpu.make_async_copy(
                            S.at[h, q], out.at[:, h, :, columns(x)], out_sem.at[h, x]
                        )
                        copy.start()
                        stores.append(copy)

        for step in range(STEPS):
            last = step + 1 == STEPS
            if step == 0:
                for copy in loads.values():
                    copy.wait()
            sends = {}
            gathers = {}
            split = len(groups) == 2
            if split:
                transport([0, 1], G + 1, depth - 2)
                for x in groups[0]:
                    first, second = moments(0, q_of(0, x)), moments(1, q_of(1, x))
                    store_moments(step, x, [a + b for a, b in zip(first, second)])
                sends[0] = send_moments(step, 0)
                transport([0, 1], Q - 1, 1)
                for h in range(2):
                    store_moments(step, plane_of(h, Q - 1), moments(h, Q - 1))
                if step == 0:
                    gathers[0] = send_coefficients(step, 0, sends[0])
                    relax_group(step, 0, gathers[0])
            else:
                transport([0, 1], G + 1, depth - 1)
                for x in range(depth):
                    total = None
                    for h in range(2):
                        if q_of(h, x) > G:
                            term = moments(h, q_of(h, x))
                            total = term if total is None else [a + b for a, b in zip(total, term)]
                    store_moments(step, x, total)

            for h in range(2):
                @pl.when(has_up[h])
                def _(h=h):
                    halo(h, step).wait_recv()
            finish_halo_send(step)
            if not last:
                start_halo(step + 1)
            for h in range(2):
                @pl.when(has_up[h])
                def _(h=h):
                    if step > 0:
                        for copy in ghost_coefficients(step - 1, h):
                            copy.wait_recv()
                    for level in range(step):
                        advance_ghost(h, G - step + level, level)

                @pl.when(jnp.logical_not(has_up[h]))
                def _(h=h):
                    fill_edge(h)

            transport([0, 1], G, 1)
            for h in range(2):
                add_moments(step, plane_of(h, G), moments(h, G))
            rim = len(groups) - 1
            sends[rim] = send_moments(step, rim)
            for g in range(len(groups)):
                if g not in gathers:
                    gathers[g] = send_coefficients(step, g, sends[g])
            for g in range(len(groups)):
                if step > 0 or g == rim:
                    relax_group(step, g, gathers[g])
            for g in range(len(groups)):
                for copy in sends[g] + gathers[g]:
                    copy.wait_send()
            if not last:
                for h in range(2):
                    @pl.when(has_down[h])
                    def _(h=h):
                        for copy in ghost_coefficients(step, h):
                            copy.wait_send()
        for copy in stores:
            copy.wait()

    dma = pltpu.SemaphoreType.DMA
    scratch = [
        pltpu.VMEM((2, Q, blocks, half, section), F32),
        pltpu.VMEM((2, Q, blocks, half, section), F32),
        pltpu.VMEM((2, Q, 8, section), F32),
        pltpu.VMEM((STEPS, FEATURES, cells), F32),
        pltpu.VMEM((STEPS, len(groups), n_vel, FEATURES, piece), F32),
        pltpu.VMEM((STEPS, COEFS, cells), F32),
        pltpu.VMEM((STEPS, 2, COEFS, (STEPS - 1) * section), F32),
        pltpu.VMEM((2, FEATURES, blocks * half), BF16),
        pltpu.VMEM((2, blocks, half, FEATURES * TERMS), BF16),
        pltpu.VMEM((2, FEATURES * TERMS, section), BF16),
        pltpu.VMEM((2, FEATURES * TERMS, section), BF16),
        pltpu.VMEM((2, blocks, half, half), F32),
        pltpu.VMEM((planes, section), jnp.int32),
        pltpu.VMEM((2, section), jnp.int32),
        pltpu.VMEM((2 * blocks, half), F32),
        dma((3,)),
        dma((2, depth)),
        dma((2, depth)),
        dma((2, STEPS)),
        dma((2, STEPS)),
        dma((STEPS, len(groups), n_vel)),
        dma((STEPS, len(groups), n_vel)),
        dma((STEPS, len(groups), n_vel)),
        dma((STEPS, len(groups), n_vel)),
        dma((STEPS, 2, STEPS)),
        dma((STEPS, 2, STEPS)),
    ]
    return kernel, scratch


def solution(mesh):
    n_vel = mesh.shape["vel"]
    n_gx = mesh.shape["gx"]

    def per_device(distribution, wall_mask, boundary_kind, inflow):
        rows, cells = distribution.shape
        section = wall_mask.shape[1]
        half = VS * VS // 2
        blocks = rows // (2 * half)
        depth = cells // section
        kernel, scratch = make_kernel(n_vel, n_gx, blocks, half, depth, section, wall_mask.shape[0])
        whole = pl.BlockSpec(memory_space=pltpu.HBM)
        out = pl.pallas_call(
            kernel,
            out_shape=jax.ShapeDtypeStruct((blocks, 2, half, cells), F32),
            in_specs=[whole] * 4,
            out_specs=whole,
            scratch_shapes=scratch,
            compiler_params=pltpu.CompilerParams(
                collective_id=0, has_side_effects=True, vmem_limit_bytes=48 * 1024 * 1024
            ),
        )(
            distribution.reshape(blocks, 2, half, cells),
            wall_mask,
            boundary_kind,
            inflow.reshape(2 * blocks, half),
        )
        return out.reshape(rows, cells)

    placed = (P("vel", "gx"), P(), P(), P("vel"))
    return jax.shard_map(
        per_device, mesh=mesh, in_specs=placed, out_specs=P("vel", "gx"), check_vma=False
    )
```

```python
import math

import jax
import jax.numpy as jnp
from jax import lax
from jax.experimental import pallas as pl
from jax.experimental.pallas import tpu as pltpu
from jax.sharding import PartitionSpec as P

VS = 16
NY = 16
NZ = 32
STEPS = 3
LANES = 128
FEATURES = 16
TERMS = 3
COEFS = 24

vel_limit = 4.5
time_step = 0.075
relax_rate = 0.6
viscous_thermal_ratio = 0.6666667
spacing = 2.0 * vel_limit / VS
unit = spacing / 2.0
MESH = pl.DeviceIdType.MESH
F32 = jnp.float32
BF16 = jnp.bfloat16


def features(index, cx, cy, cz):
    energy = cx * cx + cy * cy + cz * cz

    def high(value):
        return jnp.floor(value * (1.0 / 64.0)) * 64.0

    cubes = [energy * cx, energy * cy, energy * cz]
    rows = [jnp.ones_like(cx), cx, cy, cz, cx * cx, cy * cy, cz * cz, cx * cy, cx * cz, cy * cz]
    rows += [high(c) for c in cubes]
    rows += [c - high(c) for c in cubes]
    out = rows[0]
    for k in range(1, FEATURES):
        out = jnp.where(index == k, rows[k], out)
    return out


def shakhov_rows(moments):
    weight = spacing**3
    degree = [0, 1, 1, 1, 2, 2, 2, 2, 2, 2, 3, 3, 3]
    m = [moments[k : k + 1] for k in range(FEATURES)]
    m = m[:10] + [m[10 + a] + m[13 + a] for a in range(3)]
    m = [row * (weight * unit**d) for row, d in zip(m, degree)]
    n = m[0]
    inv_n = 1.0 / n
    u = [m[1] * inv_n, m[2] * inv_n, m[3] * inv_n]
    xx, yy, zz, xy, xz, yz = m[4:10]
    uu = u[0] * u[0] + u[1] * u[1] + u[2] * u[2]
    tr = xx + yy + zz
    temp = (tr * inv_n - uu) / 3.0
    press = [
        xx * u[0] + xy * u[1] + xz * u[2],
        xy * u[0] + yy * u[1] + yz * u[2],
        xz * u[0] + yz * u[1] + zz * u[2],
    ]
    q = [0.5 * (m[10 + a] - 2.0 * press[a] - u[a] * tr + 2.0 * n * uu * u[a]) for a in range(3)]
    inv_t = 1.0 / temp
    kappa = (1.0 - viscous_thermal_ratio) / (5.0 * n * temp * temp)
    s = kappa * inv_t
    uq = u[0] * q[0] + u[1] * q[1] + u[2] * q[2]
    first = jnp.log(n) - 1.5 * jnp.log(2.0 * math.pi * temp) - uu * (0.5 * inv_t)
    quad = -0.5 * inv_t
    expo = [first, u[0] * inv_t, u[1] * inv_t, u[2] * inv_t, quad, quad, quad]
    expo = [row * (math.log2(math.e) * unit**d) for row, d in zip(expo, [0, 1, 1, 1, 2, 2, 2])]
    poly = [1.0 - s * uq * uu + 5.0 * kappa * uq]
    poly += [s * (q[a] * uu + 2.0 * uq * u[a]) - 5.0 * kappa * q[a] for a in range(3)]
    poly += [-2.0 * s * q[a] * u[a] - s * uq for a in range(3)]
    poly += [-2.0 * s * (q[a] * u[b] + q[b] * u[a]) for a, b in ((0, 1), (0, 2), (1, 2))]
    poly += [s * q[a] for a in range(3)]
    poly = [row * (relax_rate * unit**d) for row, d in zip(poly, degree)]
    poly += poly[10:13]
    return jnp.concatenate(expo + [jnp.zeros_like(n)] + poly, axis=0)


def make_kernel(n_vel, n_gx, blocks, half, depth, section, planes):
    G = STEPS
    Q = depth + G
    cells = depth * section
    groups = [list(range(1, depth - 1)), [0, depth - 1]]
    if len(groups[0]) != len(groups[1]) or cells // 2 % (n_vel * LANES):
        groups = [list(range(depth))]
    order = [x for group in groups for x in group]
    span = cells // len(groups)
    piece = span // n_vel
    tiles = section // LANES
    wide = 2 * LANES
    zh_rows = VS // 2

    def plane_of(h, q):
        return q - G if h == 1 else depth - 1 + G - q

    def kernel(
        dist, wall_in, kind_in, inflow_in, out,
        S, M, H, PART, GOT, CO, CG, PHI, L, RP, RS, INF, wall, kind, inflow, sm_sem,
        in_sem, out_sem, hs_sem, hr_sem, ps_sem, pr_sem, cs_sem, cr_sem, gs_sem, gr_sem,
    ):
        me = lax.axis_index("vel")
        pos = lax.axis_index("gx")
        has_left = pos > 0
        has_right = pos < n_gx - 1
        has_up = [has_right, has_left]
        has_down = [has_left, has_right]
        up = [pos + 1, pos - 1]
        down = [pos - 1, pos + 1]

        def columns(x):
            return pl.ds(x * section, section)

        def place(x):
            return pl.ds(order.index(x) * section, section)

        def q_of(h, x):
            return x + G if h == 1 else depth - 1 + G - x

        loads = {}
        for q in range(Q - 1, G - 1, -1):
            for h in range(2):
                copy = pltpu.make_async_copy(
                    dist.at[:, h, :, columns(plane_of(h, q))], S.at[h, q], in_sem.at[h, q - G]
                )
                copy.start()
                loads[h, q] = copy

        small = []
        for k, (src, dst) in enumerate(((wall_in, wall), (kind_in, kind), (inflow_in, inflow))):
            copy = pltpu.make_async_copy(src, dst, sm_sem.at[k])
            copy.start()
            small.append(copy)

        barrier = pltpu.get_barrier_semaphore()
        for d in range(1, n_vel):
            pl.semaphore_signal(
                barrier, inc=1, device_id={"vel": lax.rem(me + d, n_vel)}, device_id_type=MESH
            )
        for h in range(2):
            @pl.when(has_down[h])
            def _(h=h):
                pl.semaphore_signal(barrier, inc=1, device_id={"gx": down[h]}, device_id_type=MESH)
        met = n_vel - 1 + has_left.astype(jnp.int32) + has_right.astype(jnp.int32)
        pl.semaphore_wait(barrier, met)

        def halo(h, k):
            x = depth - 1 - k if h == 1 else k
            return pltpu.make_async_remote_copy(
                src_ref=dist.at[:, h, :, columns(x)],
                dst_ref=S.at[h, G - 1 - k],
                send_sem=hs_sem.at[h, k],
                recv_sem=hr_sem.at[h, k],
                device_id={"gx": down[h]},
                device_id_type=MESH,
            )

        def start_halo(k):
            for h in range(2):
                @pl.when(has_down[h])
                def _(h=h):
                    halo(h, k).start()

        def finish_halo_send(k):
            for h in range(2):
                @pl.when(has_down[h])
                def _(h=h):
                    halo(h, k).wait_send()

        start_halo(0)

        for copy in small:
            copy.wait()

        first_iy = me * blocks
        lane = lax.broadcasted_iota(jnp.int32, (1, section), 1)
        y_at = lane // NZ
        z_at = lane % NZ
        vy_up = first_iy >= VS // 2
        n_planes = wall.shape[0]

        def openness(x):
            at = pos * depth + x
            row = wall[pl.ds(jnp.clip(at, 0, n_planes - 1), 1), :]
            inside = jnp.logical_and(at >= 0, at < n_planes)
            return jnp.where(inside, (1 - row).astype(F32), 1.0)

        for h in range(2):
            way = 1 if h == 1 else -1
            for q in range(1, Q):
                x = plane_of(h, q)
                o = openness(x)
                x_in = o * openness(x - way)
                x_out = o * openness(x + way)
                y_hi = jnp.where(y_at < NY - 1, o * pltpu.roll(o, section - NZ, 1), 0.0)
                y_lo = jnp.where(y_at > 0, o * pltpu.roll(o, NZ, 1), 0.0)
                z_hi = jnp.where(z_at < NZ - 1, o * pltpu.roll(o, section - 1, 1), 0.0)
                z_lo = jnp.where(z_at > 0, o * pltpu.roll(o, 1, 1), 0.0)
                y_in = jnp.where(vy_up, y_lo, y_hi)
                y_out = jnp.where(vy_up, y_hi, y_lo)
                rows = [x_in, x_out, y_in, y_out, z_hi, z_lo, z_lo, z_hi]
                H[h, q] = jnp.concatenate([r * time_step for r in rows], axis=0)

        for h in range(2):
            sign = 1.0 if h == 1 else -1.0
            shape = (FEATURES, blocks * half)
            r = lax.broadcasted_iota(jnp.int32, shape, 1)
            index = lax.broadcasted_iota(jnp.int32, shape, 0)
            cx = sign * (2 * ((r % half) // VS) + 1).astype(F32)
            cz = (2 * (r % VS) - (VS - 1)).astype(F32)
            cy = (2 * (first_iy + r // half) - (VS - 1)).astype(F32)
            PHI[h] = features(index, cx, cy, cz).astype(BF16)
            shape = (half, FEATURES * TERMS)
            r = lax.broadcasted_iota(jnp.int32, shape, 0)
            index = lax.broadcasted_iota(jnp.int32, shape, 1) % FEATURES
            cx = sign * (2 * (r // VS) + 1).astype(F32)
            cz = (2 * (r % VS) - (VS - 1)).astype(F32)
            for b in range(blocks):
                cy = jnp.full(shape, 2 * (first_iy + b) - (VS - 1), jnp.int32).astype(F32)
                L[h, b] = features(index, cx, cy, cz).astype(BF16)
                row = inflow[2 * b + h : 2 * b + h + 1, :]
                INF[h, b] = jnp.broadcast_to(row, (half, half)).T

        lane_t = lax.broadcasted_iota(jnp.int32, (zh_rows, LANES), 1)
        sub = lax.broadcasted_iota(jnp.int32, (zh_rows, LANES), 0).astype(F32)
        y_take = jnp.where(vy_up, LANES - NZ, 0)
        from_next = jnp.logical_and(lane_t >= y_take, lane_t < y_take + NZ)
        y_shift = jnp.where(vy_up, NZ, LANES - NZ)
        t_step = jnp.where(vy_up, tiles - 1, 1)

        def transport(h_list, q0, nq):
            nh = len(h_list)

            def body(j, carry):
                b = lax.rem(j, blocks)
                outer = lax.div(j, blocks)
                h = lax.rem(outer, nh) if nh == 2 else h_list[0]
                q = q0 + lax.div(outer, nh)
                speed_y = jnp.abs(-vel_limit + ((first_iy + b).astype(F32) + 0.5) * spacing)
                for t in range(tiles):
                    at = slice(t * LANES, (t + 1) * LANES)
                    t_next = lax.rem(t + t_step, tiles)
                    at_next = pl.ds(pl.multiple_of(t_next * LANES, LANES), LANES)

                    def face(k):
                        return jnp.broadcast_to(H[h, q, k : k + 1, at], (zh_rows, LANES))

                    x_in, x_out = face(0), face(1)
                    y_in = face(2) * speed_y
                    y_keep = 1.0 - face(3) * speed_y
                    for zh in range(2):
                        if zh == 0:
                            speed_z = vel_limit - (sub + 0.5) * spacing
                        else:
                            speed_z = (sub + 0.5) * spacing
                        z_in = face(4 + 2 * zh) * speed_z
                        keep = y_keep - face(5 + 2 * zh) * speed_z
                        for i in range(half // VS):
                            rows = pl.ds(i * VS + zh * zh_rows, zh_rows)
                            speed_x = (i + 0.5) * spacing
                            f = S[h, q, b, rows, at]
                            before = S[h, q - 1, b, rows, at]
                            beside = S[h, q, b, rows, at_next]
                            f_y = pltpu.roll(jnp.where(from_next, beside, f), y_shift, 1)
                            f_z = pltpu.roll(f, 1 if zh == 1 else LANES - 1, 1)
                            moved = f * (keep - x_out * speed_x) + before * (x_in * speed_x)
                            moved = moved + (f_y * y_in + f_z * z_in)
                            M[h, q, b, rows, at] = moved
                return carry

            lax.fori_loop(0, nh * nq * blocks, body, 0)

        def moments(h, q):
            halves = []
            for c in range(section // wide):
                value = M[h, q, :, :, c * wide : (c + 1) * wide].reshape(blocks * half, wide)
                hi = value.astype(BF16)
                lo = (value - hi.astype(F32)).astype(BF16)
                phi = PHI[h]
                halves.append(
                    jnp.dot(phi, hi, preferred_element_type=F32)
                    + jnp.dot(phi, lo, preferred_element_type=F32)
                )
            return halves

        def load_coefficients(rows, slot):
            terms = []
            rest = rows
            for j in range(TERMS):
                term = rest.astype(BF16)
                terms.append(term)
                rest = rest - term.astype(F32)
            for j in range(TERMS):
                at = slice(j * FEATURES, (j + 1) * FEATURES)
                RP[slot, at, :] = jnp.concatenate(
                    [terms[j][0:8], jnp.zeros((8, section), BF16)], axis=0
                )
                RS[slot, at, :] = terms[j][8:COEFS]

        def relax(h, q, slot):
            for c in range(section // wide):
                at = slice(c * wide, (c + 1) * wide)
                left = L[h].reshape(blocks * half, FEATURES * TERMS)
                power = jnp.dot(left, RP[slot, :, at], preferred_element_type=F32)
                shape = jnp.dot(left, RS[slot, :, at], preferred_element_type=F32)
                fresh = (jnp.exp2(power) * shape).reshape(blocks, half, wide)
                S[h, q, :, :, at] = (1.0 - relax_rate) * M[h, q, :, :, at] + fresh

        def fill_edge(h):
            inner = kind[1 - h : 2 - h, :] == 1

            for b in range(blocks):
                for t in range(tiles):
                    at = slice(t * LANES, (t + 1) * LANES)
                    S[h, G - 1, b, :, at] = jnp.where(
                        inner[:, at], INF[h, b], S[h, G, b, :, at]
                    )

        def advance_ghost(h, q, step):
            transport([h], q, 1)
            load_coefficients(CG[step, h, :, (G - 1 - q) * section : (G - q) * section], 0)
            relax(h, q, 0)

        def ghost_coefficients(step, h, sections=tuple(range(depth))):
            ghosts = STEPS - 1 - step
            if h == 1:
                parts = [depth - 1 - k for k in range(ghosts)]
            else:
                parts = list(range(ghosts))
            return [
                pltpu.make_async_remote_copy(
                    src_ref=CO.at[step, :, place(x)],
                    dst_ref=CG.at[step, h, :, columns(k)],
                    send_sem=gs_sem.at[step, h, k],
                    recv_sem=gr_sem.at[step, h, k],
                    device_id={"gx": down[h]},
                    device_id_type=MESH,
                )
                for k, x in enumerate(parts)
                if x in sections
            ]

        def share(g, who):
            return pl.ds(pl.multiple_of(g * span + who * piece, piece), piece)

        def store_moments(step, x, values):
            for c, value in enumerate(values):
                start = order.index(x) * section + c * wide
                PART[step, :, start : start + wide] = value

        def add_moments(step, x, values):
            for c, value in enumerate(values):
                start = order.index(x) * section + c * wide
                at = slice(start, start + wide)
                PART[step, :, at] = PART[step, :, at] + value

        def send_moments(step, g):
            copies = []
            for d in range(1, n_vel):
                to = lax.rem(me + d, n_vel)
                copy = pltpu.make_async_remote_copy(
                    src_ref=PART.at[step, :, share(g, to)],
                    dst_ref=GOT.at[step, g, d],
                    send_sem=ps_sem.at[step, g, d],
                    recv_sem=pr_sem.at[step, g, d],
                    device_id={"vel": to},
                    device_id_type=MESH,
                )
                copy.start()
                copies.append(copy)
            return copies

        def send_coefficients(step, g, sends):
            total = PART[step, :, share(g, me)]
            for d in range(1, n_vel):
                sends[d - 1].wait_recv()
                total = total + GOT[step, g, d]
            CO[step, :, share(g, me)] = shakhov_rows(total)
            copies = []
            for d in range(1, n_vel):
                copy = pltpu.make_async_remote_copy(
                    src_ref=CO.at[step, :, share(g, me)],
                    dst_ref=CO.at[step, :, share(g, me)],
                    send_sem=cs_sem.at[step, g, d],
                    recv_sem=cr_sem.at[step, g, d],
                    device_id={"vel": lax.rem(me + d, n_vel)},
                    device_id_type=MESH,
                )
                copy.start()
                copies.append(copy)
            return copies

        def ghost_copies(step, h, g):
            return ghost_coefficients(step, h, groups[g])

        stores = []

        def relax_group(step, g, gathers):
            for copy in gathers:
                copy.wait_recv()
            for h in range(2):
                forwards = ghost_copies(step, h, g)
                if forwards:
                    @pl.when(has_down[h])
                    def _(forwards=forwards):
                        for copy in forwards:
                            copy.start()
            for n, x in enumerate(groups[g]):
                load_coefficients(CO[step, :, place(x)], n % 2)
                for h in range(2):
                    q = q_of(h, x)
                    relax(h, q, n % 2)
                    if step + 1 == STEPS:
                        copy = pltpu.make_async_copy(
                            S.at[h, q], out.at[:, h, :, columns(x)], out_sem.at[h, x]
                        )
                        copy.start()
                        stores.append(copy)

        for step in range(STEPS):
            last = step + 1 == STEPS
            if step == 0:
                for copy in loads.values():
                    copy.wait()
            sends = {}
            gathers = {}
            split = len(groups) == 2
            if split:
                early = depth - 3 if step == 0 else 0
                transport([0, 1], G + 1, 1 + early)
                for x in groups[0]:
                    first, second = moments(0, q_of(0, x)), moments(1, q_of(1, x))
                    store_moments(step, x, [a + b for a, b in zip(first, second)])
                sends[0] = send_moments(step, 0)
                transport([0, 1], Q - 1, 1)
                for h in range(2):
                    store_moments(step, plane_of(h, Q - 1), moments(h, Q - 1))
                if step == 0:
                    gathers[0] = send_coefficients(step, 0, sends[0])
                    relax_group(step, 0, gathers[0])
            else:
                transport([0, 1], G + 1, depth - 1)
                for x in range(depth):
                    total = None
                    for h in range(2):
                        if q_of(h, x) > G:
                            term = moments(h, q_of(h, x))
                            total = term if total is None else [a + b for a, b in zip(total, term)]
                    store_moments(step, x, total)

            for h in range(2):
                @pl.when(has_up[h])
                def _(h=h):
                    halo(h, step).wait_recv()
            finish_halo_send(step)
            if not last:
                start_halo(step + 1)
            for h in range(2):
                @pl.when(has_up[h])
                def _(h=h):
                    if step > 0:
                        for copy in ghost_coefficients(step - 1, h):
                            copy.wait_recv()
                    for level in range(step):
                        advance_ghost(h, G - step + level, level)

                @pl.when(jnp.logical_not(has_up[h]))
                def _(h=h):
                    fill_edge(h)

            if split and step > 0:
                gathers[0] = send_coefficients(step, 0, sends[0])
            transport([0, 1], G, 1)
            for h in range(2):
                add_moments(step, plane_of(h, G), moments(h, G))
            rim = len(groups) - 1
            sends[rim] = send_moments(step, rim)
            if split and step > 0:
                relax_group(step, 0, gathers[0])
            gathers[rim] = send_coefficients(step, rim, sends[rim])
            if split and not last:
                transport([0, 1], G + 2, depth - 3)
            relax_group(step, rim, gathers[rim])
            for g in range(len(groups)):
                for copy in sends[g] + gathers[g]:
                    copy.wait_send()
            if not last:
                for h in range(2):
                    @pl.when(has_down[h])
                    def _(h=h):
                        for copy in ghost_coefficients(step, h):
                            copy.wait_send()
        for copy in stores:
            copy.wait()

    dma = pltpu.SemaphoreType.DMA
    scratch = [
        pltpu.VMEM((2, Q, blocks, half, section), F32),
        pltpu.VMEM((2, Q, blocks, half, section), F32),
        pltpu.VMEM((2, Q, 8, section), F32),
        pltpu.VMEM((STEPS, FEATURES, cells), F32),
        pltpu.VMEM((STEPS, len(groups), n_vel, FEATURES, piece), F32),
        pltpu.VMEM((STEPS, COEFS, cells), F32),
        pltpu.VMEM((STEPS, 2, COEFS, (STEPS - 1) * section), F32),
        pltpu.VMEM((2, FEATURES, blocks * half), BF16),
        pltpu.VMEM((2, blocks, half, FEATURES * TERMS), BF16),
        pltpu.VMEM((2, FEATURES * TERMS, section), BF16),
        pltpu.VMEM((2, FEATURES * TERMS, section), BF16),
        pltpu.VMEM((2, blocks, half, half), F32),
        pltpu.VMEM((planes, section), jnp.int32),
        pltpu.VMEM((2, section), jnp.int32),
        pltpu.VMEM((2 * blocks, half), F32),
        dma((3,)),
        dma((2, depth)),
        dma((2, depth)),
        dma((2, STEPS)),
        dma((2, STEPS)),
        dma((STEPS, len(groups), n_vel)),
        dma((STEPS, len(groups), n_vel)),
        dma((STEPS, len(groups), n_vel)),
        dma((STEPS, len(groups), n_vel)),
        dma((STEPS, 2, STEPS)),
        dma((STEPS, 2, STEPS)),
    ]
    return kernel, scratch


def solution(mesh):
    n_vel = mesh.shape["vel"]
    n_gx = mesh.shape["gx"]

    def per_device(distribution, wall_mask, boundary_kind, inflow):
        rows, cells = distribution.shape
        section = wall_mask.shape[1]
        half = VS * VS // 2
        blocks = rows // (2 * half)
        depth = cells // section
        kernel, scratch = make_kernel(n_vel, n_gx, blocks, half, depth, section, wall_mask.shape[0])
        whole = pl.BlockSpec(memory_space=pltpu.HBM)
        out = pl.pallas_call(
            kernel,
            out_shape=jax.ShapeDtypeStruct((blocks, 2, half, cells), F32),
            in_specs=[whole] * 4,
            out_specs=whole,
            scratch_shapes=scratch,
            compiler_params=pltpu.CompilerParams(
                collective_id=0, has_side_effects=True, vmem_limit_bytes=64 * 1024 * 1024
            ),
        )(
            distribution.reshape(blocks, 2, half, cells),
            wall_mask,
            boundary_kind,
            inflow.reshape(2 * blocks, half),
        )
        return out.reshape(rows, cells)

    placed = (P("vel", "gx"), P(), P(), P("vel"))
    return jax.shard_map(
        per_device, mesh=mesh, in_specs=placed, out_specs=P("vel", "gx"), check_vma=False
    )
```

```python
import math

import jax
import jax.numpy as jnp
from jax import lax
from jax.experimental import pallas as pl
from jax.experimental.pallas import tpu as pltpu
from jax.sharding import PartitionSpec as P

VS = 16
NY = 16
NZ = 32
STEPS = 3
LANES = 128
FEATURES = 16
TERMS = 3
COEFS = 24

vel_limit = 4.5
time_step = 0.075
relax_rate = 0.6
viscous_thermal_ratio = 0.6666667
spacing = 2.0 * vel_limit / VS
unit = spacing / 2.0
MESH = pl.DeviceIdType.MESH
F32 = jnp.float32
BF16 = jnp.bfloat16


def features(index, cx, cy, cz):
    energy = cx * cx + cy * cy + cz * cz

    def high(value):
        return jnp.floor(value * (1.0 / 64.0)) * 64.0

    cubes = [energy * cx, energy * cy, energy * cz]
    rows = [jnp.ones_like(cx), cx, cy, cz, cx * cx, cy * cy, cz * cz, cx * cy, cx * cz, cy * cz]
    rows += [high(c) for c in cubes]
    rows += [c - high(c) for c in cubes]
    out = rows[0]
    for k in range(1, FEATURES):
        out = jnp.where(index == k, rows[k], out)
    return out


def shakhov_rows(moments):
    weight = spacing**3
    degree = [0, 1, 1, 1, 2, 2, 2, 2, 2, 2, 3, 3, 3]
    m = [moments[k : k + 1] for k in range(FEATURES)]
    m = m[:10] + [m[10 + a] + m[13 + a] for a in range(3)]
    m = [row * (weight * unit**d) for row, d in zip(m, degree)]
    n = m[0]
    inv_n = 1.0 / n
    u = [m[1] * inv_n, m[2] * inv_n, m[3] * inv_n]
    xx, yy, zz, xy, xz, yz = m[4:10]
    uu = u[0] * u[0] + u[1] * u[1] + u[2] * u[2]
    tr = xx + yy + zz
    temp = (tr * inv_n - uu) / 3.0
    press = [
        xx * u[0] + xy * u[1] + xz * u[2],
        xy * u[0] + yy * u[1] + yz * u[2],
        xz * u[0] + yz * u[1] + zz * u[2],
    ]
    q = [0.5 * (m[10 + a] - 2.0 * press[a] - u[a] * tr + 2.0 * n * uu * u[a]) for a in range(3)]
    inv_t = 1.0 / temp
    kappa = (1.0 - viscous_thermal_ratio) / (5.0 * n * temp * temp)
    s = kappa * inv_t
    uq = u[0] * q[0] + u[1] * q[1] + u[2] * q[2]
    first = jnp.log(n) - 1.5 * jnp.log(2.0 * math.pi * temp) - uu * (0.5 * inv_t)
    quad = -0.5 * inv_t
    expo = [first, u[0] * inv_t, u[1] * inv_t, u[2] * inv_t, quad, quad, quad]
    expo = [row * (math.log2(math.e) * unit**d) for row, d in zip(expo, [0, 1, 1, 1, 2, 2, 2])]
    poly = [1.0 - s * uq * uu + 5.0 * kappa * uq]
    poly += [s * (q[a] * uu + 2.0 * uq * u[a]) - 5.0 * kappa * q[a] for a in range(3)]
    poly += [-2.0 * s * q[a] * u[a] - s * uq for a in range(3)]
    poly += [-2.0 * s * (q[a] * u[b] + q[b] * u[a]) for a, b in ((0, 1), (0, 2), (1, 2))]
    poly += [s * q[a] for a in range(3)]
    poly = [row * (relax_rate * unit**d) for row, d in zip(poly, degree)]
    poly += poly[10:13]
    return jnp.concatenate(expo + [jnp.zeros_like(n)] + poly, axis=0)


def make_kernel(n_vel, n_gx, blocks, half, depth, section, planes):
    G = STEPS
    Q = depth + G
    cells = depth * section
    groups = [list(range(1, depth - 1)), [0, depth - 1]]
    if len(groups[0]) != len(groups[1]) or cells // 2 % (n_vel * LANES):
        groups = [list(range(depth))]
    order = [x for group in groups for x in group]
    span = cells // len(groups)
    piece = span // n_vel
    tiles = section // LANES
    wide = 2 * LANES
    zh_rows = VS // 2

    def plane_of(h, q):
        return q - G if h == 1 else depth - 1 + G - q

    def kernel(
        dist, small, out,
        S, M, H, PART, GOT, CO, CG, PHI, L, RP, RS, INF,
        in_sem, out_sem, hs_sem, hr_sem, ps_sem, pr_sem, cs_sem, cr_sem, gs_sem, gr_sem,
    ):
        me = lax.axis_index("vel")
        pos = lax.axis_index("gx")
        has_left = pos > 0
        has_right = pos < n_gx - 1
        has_up = [has_right, has_left]
        has_down = [has_left, has_right]
        up = [pos + 1, pos - 1]
        down = [pos - 1, pos + 1]

        def columns(x):
            return pl.ds(x * section, section)

        def place(x):
            return pl.ds(order.index(x) * section, section)

        def q_of(h, x):
            return x + G if h == 1 else depth - 1 + G - x

        loads = {}
        for q in range(Q - 1, G - 1, -1):
            for h in range(2):
                copy = pltpu.make_async_copy(
                    dist.at[:, h, :, columns(plane_of(h, q))], S.at[h, q], in_sem.at[h, q - G]
                )
                copy.start()
                loads[h, q] = copy

        barrier = pltpu.get_barrier_semaphore()
        for d in range(1, n_vel):
            pl.semaphore_signal(
                barrier, inc=1, device_id={"vel": lax.rem(me + d, n_vel)}, device_id_type=MESH
            )
        for h in range(2):
            @pl.when(has_down[h])
            def _(h=h):
                pl.semaphore_signal(barrier, inc=1, device_id={"gx": down[h]}, device_id_type=MESH)
        met = n_vel - 1 + has_left.astype(jnp.int32) + has_right.astype(jnp.int32)
        pl.semaphore_wait(barrier, met)

        def halo(h, k):
            x = depth - 1 - k if h == 1 else k
            return pltpu.make_async_remote_copy(
                src_ref=dist.at[:, h, :, columns(x)],
                dst_ref=S.at[h, G - 1 - k],
                send_sem=hs_sem.at[h, k],
                recv_sem=hr_sem.at[h, k],
                device_id={"gx": down[h]},
                device_id_type=MESH,
            )

        def start_halo(k):
            for h in range(2):
                @pl.when(has_down[h])
                def _(h=h):
                    halo(h, k).start()

        def finish_halo_send(k):
            for h in range(2):
                @pl.when(has_down[h])
                def _(h=h):
                    halo(h, k).wait_send()

        start_halo(0)

        first_iy = me * blocks
        lane = lax.broadcasted_iota(jnp.int32, (1, section), 1)
        y_at = lane // NZ
        z_at = lane % NZ
        vy_up = first_iy >= VS // 2

        def openness(x):
            at = pos * depth + x
            row = small[pl.ds(jnp.clip(at, 0, planes - 1), 1), :]
            inside = jnp.logical_and(at >= 0, at < planes)
            return jnp.where(inside, 1.0 - row, 1.0)

        for h in range(2):
            way = 1 if h == 1 else -1
            for q in range(1, Q):
                x = plane_of(h, q)
                o = openness(x)
                x_in = o * openness(x - way)
                x_out = o * openness(x + way)
                y_hi = jnp.where(y_at < NY - 1, o * pltpu.roll(o, section - NZ, 1), 0.0)
                y_lo = jnp.where(y_at > 0, o * pltpu.roll(o, NZ, 1), 0.0)
                z_hi = jnp.where(z_at < NZ - 1, o * pltpu.roll(o, section - 1, 1), 0.0)
                z_lo = jnp.where(z_at > 0, o * pltpu.roll(o, 1, 1), 0.0)
                y_in = jnp.where(vy_up, y_lo, y_hi)
                y_out = jnp.where(vy_up, y_hi, y_lo)
                rows = [x_in, x_out, y_in, y_out, z_hi, z_lo, z_lo, z_hi]
                H[h, q] = jnp.concatenate([r * time_step for r in rows], axis=0)

        for h in range(2):
            sign = 1.0 if h == 1 else -1.0
            shape = (FEATURES, blocks * half)
            r = lax.broadcasted_iota(jnp.int32, shape, 1)
            index = lax.broadcasted_iota(jnp.int32, shape, 0)
            cx = sign * (2 * ((r % half) // VS) + 1).astype(F32)
            cz = (2 * (r % VS) - (VS - 1)).astype(F32)
            cy = (2 * (first_iy + r // half) - (VS - 1)).astype(F32)
            PHI[h] = features(index, cx, cy, cz).astype(BF16)
            shape = (half, FEATURES * TERMS)
            r = lax.broadcasted_iota(jnp.int32, shape, 0)
            index = lax.broadcasted_iota(jnp.int32, shape, 1) % FEATURES
            cx = sign * (2 * (r // VS) + 1).astype(F32)
            cz = (2 * (r % VS) - (VS - 1)).astype(F32)
            for b in range(blocks):
                cy = jnp.full(shape, 2 * (first_iy + b) - (VS - 1), jnp.int32).astype(F32)
                L[h, b] = features(index, cx, cy, cz).astype(BF16)
                start = (2 * b + h) * half
                line = planes + 2 + start // section
                row = small[line : line + 1, start % section : start % section + half]
                INF[h, b] = jnp.broadcast_to(row, (half, half)).T

        lane_t = lax.broadcasted_iota(jnp.int32, (zh_rows, LANES), 1)
        sub = lax.broadcasted_iota(jnp.int32, (zh_rows, LANES), 0).astype(F32)
        y_take = jnp.where(vy_up, LANES - NZ, 0)
        from_next = jnp.logical_and(lane_t >= y_take, lane_t < y_take + NZ)
        y_shift = jnp.where(vy_up, NZ, LANES - NZ)
        t_step = jnp.where(vy_up, tiles - 1, 1)

        def transport(h_list, q0, nq):
            nh = len(h_list)

            def body(j, carry):
                b = lax.rem(j, blocks)
                outer = lax.div(j, blocks)
                h = lax.rem(outer, nh) if nh == 2 else h_list[0]
                q = q0 + lax.div(outer, nh)
                speed_y = jnp.abs(-vel_limit + ((first_iy + b).astype(F32) + 0.5) * spacing)
                for t in range(tiles):
                    at = slice(t * LANES, (t + 1) * LANES)
                    t_next = lax.rem(t + t_step, tiles)
                    at_next = pl.ds(pl.multiple_of(t_next * LANES, LANES), LANES)

                    def face(k):
                        return jnp.broadcast_to(H[h, q, k : k + 1, at], (zh_rows, LANES))

                    x_in, x_out = face(0), face(1)
                    y_in = face(2) * speed_y
                    y_keep = 1.0 - face(3) * speed_y
                    for zh in range(2):
                        if zh == 0:
                            speed_z = vel_limit - (sub + 0.5) * spacing
                        else:
                            speed_z = (sub + 0.5) * spacing
                        z_in = face(4 + 2 * zh) * speed_z
                        keep = y_keep - face(5 + 2 * zh) * speed_z
                        for i in range(half // VS):
                            rows = pl.ds(i * VS + zh * zh_rows, zh_rows)
                            speed_x = (i + 0.5) * spacing
                            f = S[h, q, b, rows, at]
                            before = S[h, q - 1, b, rows, at]
                            beside = S[h, q, b, rows, at_next]
                            f_y = pltpu.roll(jnp.where(from_next, beside, f), y_shift, 1)
                            f_z = pltpu.roll(f, 1 if zh == 1 else LANES - 1, 1)
                            moved = f * (keep - x_out * speed_x) + before * (x_in * speed_x)
                            moved = moved + (f_y * y_in + f_z * z_in)
                            M[h, q, b, rows, at] = moved
                return carry

            lax.fori_loop(0, nh * nq * blocks, body, 0)

        def moments(h, q):
            halves = []
            for c in range(section // wide):
                value = M[h, q, :, :, c * wide : (c + 1) * wide].reshape(blocks * half, wide)
                hi = value.astype(BF16)
                lo = (value - hi.astype(F32)).astype(BF16)
                phi = PHI[h]
                halves.append(
                    jnp.dot(phi, hi, preferred_element_type=F32)
                    + jnp.dot(phi, lo, preferred_element_type=F32)
                )
            return halves

        def load_coefficients(rows, slot):
            terms = []
            rest = rows
            for j in range(TERMS):
                term = rest.astype(BF16)
                terms.append(term)
                rest = rest - term.astype(F32)
            for j in range(TERMS):
                at = slice(j * FEATURES, (j + 1) * FEATURES)
                RP[slot, at, :] = jnp.concatenate(
                    [terms[j][0:8], jnp.zeros((8, section), BF16)], axis=0
                )
                RS[slot, at, :] = terms[j][8:COEFS]

        def relax(h, q, slot):
            for c in range(section // wide):
                at = slice(c * wide, (c + 1) * wide)
                left = L[h].reshape(blocks * half, FEATURES * TERMS)
                power = jnp.dot(left, RP[slot, :, at], preferred_element_type=F32)
                shape = jnp.dot(left, RS[slot, :, at], preferred_element_type=F32)
                fresh = (jnp.exp2(power) * shape).reshape(blocks, half, wide)
                S[h, q, :, :, at] = (1.0 - relax_rate) * M[h, q, :, :, at] + fresh

        def fill_edge(h):
            inner = small[planes + 1 - h : planes + 2 - h, :] == 1.0

            for b in range(blocks):
                for t in range(tiles):
                    at = slice(t * LANES, (t + 1) * LANES)
                    S[h, G - 1, b, :, at] = jnp.where(
                        inner[:, at], INF[h, b], S[h, G, b, :, at]
                    )

        def advance_ghost(h, q, step):
            transport([h], q, 1)
            load_coefficients(CG[step, h, :, (G - 1 - q) * section : (G - q) * section], 0)
            relax(h, q, 0)

        def ghost_coefficients(step, h, sections=tuple(range(depth))):
            ghosts = STEPS - 1 - step
            if h == 1:
                parts = [depth - 1 - k for k in range(ghosts)]
            else:
                parts = list(range(ghosts))
            return [
                pltpu.make_async_remote_copy(
                    src_ref=CO.at[step, :, place(x)],
                    dst_ref=CG.at[step, h, :, columns(k)],
                    send_sem=gs_sem.at[step, h, k],
                    recv_sem=gr_sem.at[step, h, k],
                    device_id={"gx": down[h]},
                    device_id_type=MESH,
                )
                for k, x in enumerate(parts)
                if x in sections
            ]

        def share(g, who):
            return pl.ds(pl.multiple_of(g * span + who * piece, piece), piece)

        def store_moments(step, x, values):
            for c, value in enumerate(values):
                start = order.index(x) * section + c * wide
                PART[step, :, start : start + wide] = value

        def add_moments(step, x, values):
            for c, value in enumerate(values):
                start = order.index(x) * section + c * wide
                at = slice(start, start + wide)
                PART[step, :, at] = PART[step, :, at] + value

        def send_moments(step, g):
            copies = []
            for d in range(1, n_vel):
                to = lax.rem(me + d, n_vel)
                copy = pltpu.make_async_remote_copy(
                    src_ref=PART.at[step, :, share(g, to)],
                    dst_ref=GOT.at[step, g, d],
                    send_sem=ps_sem.at[step, g, d],
                    recv_sem=pr_sem.at[step, g, d],
                    device_id={"vel": to},
                    device_id_type=MESH,
                )
                copy.start()
                copies.append(copy)
            return copies

        def send_coefficients(step, g, sends):
            total = PART[step, :, share(g, me)]
            for d in range(1, n_vel):
                sends[d - 1].wait_recv()
                total = total + GOT[step, g, d]
            CO[step, :, share(g, me)] = shakhov_rows(total)
            copies = []
            for d in range(1, n_vel):
                copy = pltpu.make_async_remote_copy(
                    src_ref=CO.at[step, :, share(g, me)],
                    dst_ref=CO.at[step, :, share(g, me)],
                    send_sem=cs_sem.at[step, g, d],
                    recv_sem=cr_sem.at[step, g, d],
                    device_id={"vel": lax.rem(me + d, n_vel)},
                    device_id_type=MESH,
                )
                copy.start()
                copies.append(copy)
            return copies

        def ghost_copies(step, h, g):
            return ghost_coefficients(step, h, groups[g])

        stores = []

        def relax_group(step, g, gathers):
            for copy in gathers:
                copy.wait_recv()
            for h in range(2):
                forwards = ghost_copies(step, h, g)
                if forwards:
                    @pl.when(has_down[h])
                    def _(forwards=forwards):
                        for copy in forwards:
                            copy.start()
            for n, x in enumerate(groups[g]):
                load_coefficients(CO[step, :, place(x)], n % 2)
                for h in range(2):
                    q = q_of(h, x)
                    relax(h, q, n % 2)
                    if step + 1 == STEPS:
                        copy = pltpu.make_async_copy(
                            S.at[h, q], out.at[:, h, :, columns(x)], out_sem.at[h, x]
                        )
                        copy.start()
                        stores.append(copy)

        for step in range(STEPS):
            last = step + 1 == STEPS
            if step == 0:
                for copy in loads.values():
                    copy.wait()
            sends = {}
            gathers = {}
            split = len(groups) == 2
            if split:
                early = depth - 3 if step == 0 else 0
                transport([0, 1], G + 1, 1 + early)
                for x in groups[0]:
                    first, second = moments(0, q_of(0, x)), moments(1, q_of(1, x))
                    store_moments(step, x, [a + b for a, b in zip(first, second)])
                sends[0] = send_moments(step, 0)
                if step > 0 and not last:
                    start_halo(step + 1)
                transport([0, 1], Q - 1, 1)
                for h in range(2):
                    store_moments(step, plane_of(h, Q - 1), moments(h, Q - 1))
                if step == 0:
                    gathers[0] = send_coefficients(step, 0, sends[0])
                    relax_group(step, 0, gathers[0])
            else:
                transport([0, 1], G + 1, depth - 1)
                for x in range(depth):
                    total = None
                    for h in range(2):
                        if q_of(h, x) > G:
                            term = moments(h, q_of(h, x))
                            total = term if total is None else [a + b for a, b in zip(total, term)]
                    store_moments(step, x, total)

            for h in range(2):
                @pl.when(has_up[h])
                def _(h=h):
                    halo(h, step).wait_recv()
            finish_halo_send(step)
            if step == 0 or not (last or split):
                start_halo(step + 1)
            for h in range(2):
                @pl.when(has_up[h])
                def _(h=h):
                    if step > 0:
                        for copy in ghost_coefficients(step - 1, h):
                            copy.wait_recv()
                    for level in range(step):
                        advance_ghost(h, G - step + level, level)

                @pl.when(jnp.logical_not(has_up[h]))
                def _(h=h):
                    fill_edge(h)

            if split and step > 0:
                gathers[0] = send_coefficients(step, 0, sends[0])
            transport([0, 1], G, 1)
            for h in range(2):
                add_moments(step, plane_of(h, G), moments(h, G))
            rim = len(groups) - 1
            sends[rim] = send_moments(step, rim)
            if split and step > 0:
                relax_group(step, 0, gathers[0])
            gathers[rim] = send_coefficients(step, rim, sends[rim])
            if split and not last:
                transport([0, 1], G + 2, depth - 3)
            relax_group(step, rim, gathers[rim])
            for g in range(len(groups)):
                for copy in sends[g] + gathers[g]:
                    copy.wait_send()
            if not last:
                for h in range(2):
                    @pl.when(has_down[h])
                    def _(h=h):
                        for copy in ghost_coefficients(step, h):
                            copy.wait_send()
        for copy in stores:
            copy.wait()

    dma = pltpu.SemaphoreType.DMA
    scratch = [
        pltpu.VMEM((2, Q, blocks, half, section), F32),
        pltpu.VMEM((2, Q, blocks, half, section), F32),
        pltpu.VMEM((2, Q, 8, section), F32),
        pltpu.VMEM((STEPS, FEATURES, cells), F32),
        pltpu.VMEM((STEPS, len(groups), n_vel, FEATURES, piece), F32),
        pltpu.VMEM((STEPS, COEFS, cells), F32),
        pltpu.VMEM((STEPS, 2, COEFS, (STEPS - 1) * section), F32),
        pltpu.VMEM((2, FEATURES, blocks * half), BF16),
        pltpu.VMEM((2, blocks, half, FEATURES * TERMS), BF16),
        pltpu.VMEM((2, FEATURES * TERMS, section), BF16),
        pltpu.VMEM((2, FEATURES * TERMS, section), BF16),
        pltpu.VMEM((2, blocks, half, half), F32),
        dma((2, depth)),
        dma((2, depth)),
        dma((2, STEPS)),
        dma((2, STEPS)),
        dma((STEPS, len(groups), n_vel)),
        dma((STEPS, len(groups), n_vel)),
        dma((STEPS, len(groups), n_vel)),
        dma((STEPS, len(groups), n_vel)),
        dma((STEPS, 2, STEPS)),
        dma((STEPS, 2, STEPS)),
    ]
    return kernel, scratch


def solution(mesh):
    n_vel = mesh.shape["vel"]
    n_gx = mesh.shape["gx"]

    def per_device(distribution, wall_mask, boundary_kind, inflow):
        rows, cells = distribution.shape
        section = wall_mask.shape[1]
        half = VS * VS // 2
        blocks = rows // (2 * half)
        depth = cells // section
        kernel, scratch = make_kernel(n_vel, n_gx, blocks, half, depth, section, wall_mask.shape[0])
        entering = jnp.pad(inflow, (0, -rows % section)).reshape(-1, section)
        small = jnp.concatenate(
            [wall_mask.astype(F32), boundary_kind.astype(F32), entering], axis=0
        )
        whole = pl.BlockSpec(memory_space=pltpu.HBM)
        out = pl.pallas_call(
            kernel,
            out_shape=jax.ShapeDtypeStruct((blocks, 2, half, cells), F32),
            in_specs=[whole, pl.BlockSpec(memory_space=pltpu.VMEM)],
            out_specs=whole,
            scratch_shapes=scratch,
            compiler_params=pltpu.CompilerParams(
                collective_id=0, has_side_effects=True, vmem_limit_bytes=48 * 1024 * 1024
            ),
        )(
            distribution.reshape(blocks, 2, half, cells),
            small,
        )
        return out.reshape(rows, cells)

    placed = (P("vel", "gx"), P(), P(), P("vel"))
    return jax.shard_map(
        per_device, mesh=mesh, in_specs=placed, out_specs=P("vel", "gx"), check_vma=False
    )
```
